256 devices in a mesh: dev: 256 (over y, z, x, core).
Axes of the slice: x: 4, y: 4, z: 8, core: 2. Of those that a mesh axis runs over, the one named last changes fastest.
Arguments:
- states: bfloat16 [1024, 4096], P('dev'), may hold values from -24 to 24
- head_weight: bfloat16 [4096, 1024], replicated, may hold values from -0.25 to 0.25
- bank: bfloat16 [262144, 1024], P('dev'), may hold values from -8 to 8
- positive_index: int32 [1024], P('dev'), may hold values from 0 to 262143
Outputs:
- loss: float32 [], replicated
- top_score: float32 [1024], P('dev')
- grad_states: bfloat16 [1024, 4096], P('dev')
- grad_weight: float32 [4096, 1024], P('dev')
The draws below stay inside these ranges and needn't reach their ends.
All inputs are finite; a program needn't handle non-finite values.
Results may differ from the reference program's by a relative error of at most 0.012.
The reference program's roundings to bfloat16 on the way (of `query`, `coef` and `grad_projected`) count: a program that leaves them out, or rounds other values in their place, can miss the bound.
Values may be sent and summed in bfloat16 or wider, within the bound.
A program may use at most 128 MiB of HBM per device.

```python
import jax
import jax.numpy as jnp
from jax import lax

H = 4096
E = 1024
BANK_DEV = 1024
QUERIES = 1024
BANK = 262144
N_DEV = 256


def draw_head_weight(key, part):
    key = jax.random.fold_in(key, 11)
    noise_key = jax.random.fold_in(key, 0)
    values = jnp.clip(jax.random.normal(noise_key, (H, E), jnp.float32), -4.0, 4.0) * H ** (-0.5)
    return jnp.clip(values, -0.25, 0.25).astype(jnp.bfloat16)


def draw_bank(key, part):
    key = jax.random.fold_in(key, 23)
    subkeys = jax.random.split(key, 3)
    row_numbers = jnp.arange(BANK).astype(jnp.int32)
    rising = 1.0 + 2.0 * row_numbers.astype(jnp.float32) / max(BANK - 1, 1)
    row_scale = jax.random.uniform(subkeys[0], (BANK,), jnp.float32, jnp.log(0.03), jnp.log(0.3))
    row_scale = jnp.exp(row_scale) * rising
    col_scale = jnp.exp(jax.random.uniform(subkeys[1], (E,), jnp.float32, jnp.log(0.5), jnp.log(2.0)))
    background = jnp.clip(jax.random.normal(subkeys[2], (BANK, E), jnp.float32), -4.0, 4.0)
    values = background * row_scale[:, None] * col_scale[None, :]
    return jnp.clip(values, -8.0, 8.0).astype(jnp.bfloat16)


def touch_ends(result, rng, smallest, high):
    extent = result.shape
    place = [jax.random.randint(jax.random.fold_in(rng, axis), (), 0, extent[axis]) for axis in range(len(extent))]
    result = result.at[tuple(place)].set(smallest)
    longest = extent.index(max(extent))
    place[longest] = (place[longest] + 1) % extent[longest]
    return result.at[tuple(place)].set(high)


def with_spikes(result, stream_key, source, target, shards_of, factor):
    owner, partner = [(jnp.arange(result.shape[axis_at]) // (result.shape[axis_at] // shards_of)).reshape([-1 if axis == axis_at else 1 for axis in range(result.ndim)]) for axis_at in (source, target)]
    chosen = jax.random.permutation(stream_key, shards_of)[partner]
    strong = (owner == chosen) | (owner == (partner + shards_of // 2) % shards_of)
    return jnp.where(strong, factor * result, result)


def levels(stream_key, dims, cuts, smallest, largest):
    factor_of, own = 1.0, jax.random.fold_in(stream_key, 6)
    for dim, shards_of in cuts:
        heights = jnp.exp(jax.random.uniform(jax.random.fold_in(own, dim), (shards_of,), jnp.float32, smallest / len(cuts), largest / len(cuts)))
        factor_of = factor_of * jnp.repeat(heights, dims[dim] // shards_of).reshape([-1 if axis == dim else 1 for axis in range(len(dims))])
    return factor_of


def heavy_noise(key, extent, width, reach, cuts, heavy, held_as=jnp.bfloat16):
    drawn = width * jax.random.normal(key, extent, jnp.float32)
    if cuts:
        drawn = drawn * levels(key, extent, cuts, -0.22, 0.18)
    return jnp.clip(with_spikes(drawn, jax.random.fold_in(key, 3), *heavy), -reach, reach).astype(held_as)


def setup_inputs(seed: int = 0) -> dict:
    streams_of = jax.random.split(jax.random.key(seed), 5)
    return {
        "states": heavy_noise(streams_of[0], (QUERIES, H), 1.0, 24.0, ((0, 256),), (0, 1, 256, 6.0)),
        "head_weight": draw_head_weight(jax.random.fold_in(streams_of[4], 71), 0),
        "bank": draw_bank(jax.random.fold_in(streams_of[4], 71), 0),
        "positive_index": touch_ends(jax.random.randint(streams_of[3], (QUERIES,), 0, BANK), jax.random.fold_in(streams_of[3], 1), 0, BANK - 1).astype(jnp.int32),
    }


def reference(states, head_weight, bank, positive_index):
    projected = jnp.dot(states, head_weight, preferred_element_type=jnp.float32)
    radius = jnp.sqrt(lax.optimization_barrier(jnp.sum(projected * projected, axis=1, keepdims=True)) + 1e-06)
    unit = projected / radius
    query = unit.astype(jnp.bfloat16)
    blocks = bank.reshape(N_DEV, BANK_DEV, E)
    starts = (jnp.arange(N_DEV) * BANK_DEV).astype(jnp.int32)
    columns = jnp.arange(BANK_DEV).astype(jnp.int32)

    def block_scores(block):
        return 20.0 * jnp.dot(query, block.T, preferred_element_type=jnp.float32)

    def first_pass(carry, item):
        block, start = item
        top, total, positive = carry
        scores = block_scores(block)
        hits = (positive_index - start)[:, None] == columns[None, :]
        new_top = jnp.maximum(top, lax.optimization_barrier(jnp.max(scores, axis=1)))
        total = total * jnp.exp(top - new_top) + lax.optimization_barrier(jnp.sum(jnp.exp(scores - new_top[:, None]), axis=1))
        positive = positive + lax.optimization_barrier(jnp.sum(jnp.where(hits, scores, 0.0), axis=1))
        return ((new_top, total, positive), None)
    begin = (jnp.full((QUERIES,), -jnp.inf, jnp.float32), jnp.zeros((QUERIES,), jnp.float32), jnp.zeros((QUERIES,), jnp.float32))
    (top_score, total, positive), _ = lax.scan(first_pass, begin, (blocks, starts))
    lse = top_score + jnp.log(total)
    loss = jnp.mean(lse - positive)

    def second_pass(carry, item):
        block, start = item
        scores = block_scores(block)
        hits = ((positive_index - start)[:, None] == columns[None, :]).astype(jnp.float32)
        coef = ((jnp.exp(scores - lse[:, None]) - hits) / QUERIES).astype(jnp.bfloat16)
        return (carry + 20.0 * jnp.dot(coef, block, preferred_element_type=jnp.float32), None)
    grad_query, _ = lax.scan(second_pass, jnp.zeros((QUERIES, E), jnp.float32), (blocks, starts))
    inner = lax.optimization_barrier(jnp.sum(unit * grad_query, axis=1, keepdims=True))
    grad_projected = ((grad_query - unit * inner) / radius).astype(jnp.bfloat16)
    grad_states = jnp.dot(grad_projected, head_weight.T, preferred_element_type=jnp.float32).astype(jnp.bfloat16)
    grad_weight = jnp.dot(states.T, grad_projected, preferred_element_type=jnp.float32)
    return (loss, top_score, grad_states, grad_weight)
```

```python
import functools

import jax
import jax.numpy as jnp
from jax import lax
from jax.experimental import pallas as pl
from jax.experimental.pallas import tpu as pltpu
from jax.sharding import PartitionSpec as P

NY, NZ, NX = 4, 8, 4
PLANE = NY * NX
OWN = 4
H, E = 4096, 1024
BANK = 1024
BLOCK = NZ * OWN
CHUNK = NX * BLOCK
ROWS = NY * CHUNK
LANES = 128
SPLIT = E // LANES
W_PARTS = 8
QUERIES = 1024
MESH = pl.DeviceIdType.MESH
NT = (((1,), (1,)), ((), ()))
POS, STATES, QUERY, STATS, GRAD, PROJ = range(6)
F32, BF16 = jnp.float32, jnp.bfloat16


def kernel(
    states_ref, w_hbm, bank_hbm, pos_ref,
    loss_ref, top_ref, gs_ref, gw_ref,
    w, bank, posz, posp, stz_out, stz_in, stp_out, slab, slab_t, turn,
    zq, unit_s, radius_s, qall, expo, coef, sp, sz, final, gout, gin,
    gz_out, gz_in, zg, own_gp, gpall, gw_acc, gw_in, lossbuf,
    w_sem, bank_sem, cs, cr, zs, zr, ps, pr,
):
    me = lax.axis_index("dev")
    c = lax.rem(me, 2)
    x = lax.rem(me // 2, NX)
    z = lax.rem(me // (2 * NX), NZ)
    y = me // (2 * NX * NZ)
    p = y * NX + x
    chip = me // 2
    partner = chip * 2 + (1 - c)

    def dev(yy, zz, xx):
        return ((yy * NZ + zz) * NX + xx) * 2 + c

    def rows(i, n):
        return pl.ds(pl.multiple_of(i * n, n), n)

    def z_copy(stage, t, src, dst, slot):
        return pltpu.make_async_remote_copy(
            src_ref=src, dst_ref=dst, send_sem=zs.at[stage, t], recv_sem=zr.at[stage, slot],
            device_id=(dev(y, t, x),), device_id_type=MESH,
        )

    def p_copy(stage, t, src, dst, slot):
        return pltpu.make_async_remote_copy(
            src_ref=src, dst_ref=dst, send_sem=ps.at[stage, t], recv_sem=pr.at[stage, slot],
            device_id=(dev(t // NX, z, lax.rem(t, NX)),), device_id_type=MESH,
        )

    def z_each(body):
        def step(k, carry):
            body(lax.rem(z + k, NZ))
            return carry
        lax.fori_loop(1, NZ, step, 0)

    def p_peer(k):
        return lax.rem(y + k // NX, NY) * NX + lax.rem(x + lax.rem(k, NX), NX)

    def p_each(body, first=1, last=PLANE):
        def step(k, carry):
            body(p_peer(k))
            return carry
        lax.fori_loop(first, last, step, 0)

    def z_send(stage, src, dst):
        z_each(lambda t: z_copy(stage, t, src(t), dst(z), z).start())

    def z_recv(stage, dst):
        z_each(lambda t: z_copy(stage, t, dst(t), dst(t), t).wait_recv())

    def z_drain(stage, src):
        z_each(lambda t: z_copy(stage, t, src(t), src(t), t).wait_send())

    def p_send(stage, src, dst):
        p_each(lambda t: p_copy(stage, t, src(t), dst(p), p).start())

    def p_recv(stage, dst, first=1, last=PLANE):
        p_each(lambda t: p_copy(stage, t, dst(t), dst(t), t).wait_recv(), first, last)

    def p_drain(stage, src):
        p_each(lambda t: p_copy(stage, t, src(t), src(t), t).wait_send())

    def w_copy(i):
        part = pl.ds(i * (H // W_PARTS), H // W_PARTS)
        return pltpu.make_async_copy(w_hbm.at[part, :], w.at[part, :], w_sem.at[i])

    for i in range(W_PARTS):
        w_copy(i).start()
    mine = rows(c, BANK)
    other = rows(1 - c, BANK)
    own_bank = pltpu.make_async_copy(bank_hbm, bank.at[mine, :], bank_sem)
    own_bank.start()

    barrier = pltpu.get_barrier_semaphore()

    def greet(target):
        pl.semaphore_signal(barrier, inc=1, device_id=(target,), device_id_type=MESH)

    greet(partner)
    z_each(lambda t: greet(dev(y, t, x)))
    p_each(lambda t: greet(dev(t // NX, z, lax.rem(t, NX))))
    lane = lax.broadcasted_iota(jnp.int32, (8, LANES), 1)
    sub = lax.broadcasted_iota(jnp.int32, (8, LANES), 0)
    first_lane = x * BLOCK + z * OWN
    tile = jnp.zeros((8, LANES), jnp.int32)
    for r in range(OWN):
        tile = jnp.where((lane == first_lane + r) & (sub == y), pos_ref[r], tile)
    posz[rows(z, 8), :] = tile
    states_f = states_ref[...].astype(F32)
    for zz in range(NZ):
        for yy in range(NY):
            at = (yy * NZ + zz) * LANES
            stz_out[pl.ds(zz * 16 + yy, OWN, stride=NY), :] = states_f[:, at:at + LANES]
    pl.semaphore_wait(barrier, 1 + (NZ - 1) + (PLANE - 1))

    def core_copy(i, src, dst):
        return pltpu.make_async_remote_copy(
            src_ref=src, dst_ref=dst, send_sem=cs.at[i], recv_sem=cr.at[i],
            device_id=(partner,), device_id_type=MESH,
        )

    bank_out = core_copy(0, bank_hbm, bank.at[mine, :])
    bank_out.start()

    z_send(POS, lambda t: posz.at[rows(z, 8), :], lambda s: posz.at[rows(s, 8), :])
    stz_in[rows(z, 16), :] = stz_out[rows(z, 16), :]
    z_send(STATES, lambda t: stz_out.at[rows(t, 16), :], lambda s: stz_in.at[rows(s, 16), :])

    proj = jnp.zeros((OWN, E), F32)
    for i in range(W_PARTS):
        w_copy(i).wait()
        part = slice(i * (H // W_PARTS), (i + 1) * (H // W_PARTS))
        proj = proj + jnp.dot(states_ref[:, part], w[part, :], preferred_element_type=F32)
    radius = jnp.sqrt(jnp.sum(proj * proj, axis=1, keepdims=True) + 1e-06)
    unit = proj / radius
    for e in range(SPLIT):
        unit_s[pl.ds(e, OWN, stride=SPLIT), :] = unit[:, e * LANES:(e + 1) * LANES]
    radius_b = jnp.broadcast_to(radius, (OWN, LANES))
    for e in range(SPLIT):
        radius_s[pl.ds(e, OWN, stride=SPLIT), :] = radius_b
    zq[rows(z, BLOCK), :] = unit_s[...]
    zq_at = lambda s: zq.at[rows(s, BLOCK), :]
    z_send(QUERY, lambda t: zq_at(z), zq_at)

    z_recv(POS, lambda s: posz.at[rows(s, 8), :])
    tile = jnp.zeros((8, LANES), jnp.int32)
    for s in range(NZ):
        tile = tile + posz[s * 8:(s + 1) * 8, :]
    posp[rows(p, 8), :] = tile
    posp_at = lambda s: posp.at[rows(s, 8), :]
    p_send(POS, lambda t: posp_at(p), posp_at)
    z_recv(STATES, lambda s: stz_in.at[rows(s, 16), :])
    for yy in range(NY):
        stp_out[yy * BLOCK:(yy + 1) * BLOCK, :] = stz_in[pl.ds(yy, BLOCK, stride=NY), :].astype(BF16)
    block_at = lambda ref: (lambda s: ref.at[rows(s, BLOCK), :])
    st_src = lambda t: stp_out.at[rows(t // NX, BLOCK), :]

    z_recv(QUERY, zq_at)

    def assemble(zbuf, target):
        for e in range(SPLIT):
            target[rows(p, BLOCK), e * LANES:(e + 1) * LANES] = zbuf[pl.ds(e, BLOCK, stride=SPLIT), :].astype(BF16)

    assemble(zq, qall)
    p_send(QUERY, lambda t: block_at(qall)(p), block_at(qall))
    p_send(STATES, st_src, block_at(slab))
    slab[rows(p, BLOCK), :] = stp_out[rows(y, BLOCK), :]
    own_bank.wait()
    core_copy(0, bank.at[other, :], bank.at[other, :]).wait_recv()
    p_recv(POS, posp_at)
    tile = jnp.zeros((8, LANES), jnp.int32)
    for s in range(PLANE):
        tile = tile + posp[s * 8:(s + 1) * 8, :]
    final[16:24, :] = (tile - chip * (2 * BANK)).astype(F32)

    eye = lax.broadcasted_iota(jnp.int32, (LANES, LANES), 0) == lax.broadcasted_iota(jnp.int32, (LANES, LANES), 1)
    to_row = lambda col: jnp.sum(jnp.where(eye, jnp.broadcast_to(col, (LANES, LANES)), 0.0), axis=0, keepdims=True)
    to_col = lambda row: jnp.sum(jnp.where(eye, jnp.broadcast_to(row, (LANES, LANES)), 0.0), axis=1, keepdims=True)
    TILE = 512
    tiles = 2 * BANK // TILE
    column = lax.broadcasted_iota(jnp.int32, (CHUNK, TILE), 1)

    sp[rows(p, 16), :] = jnp.zeros((16, LANES), F32)

    def score_chunk(k, carry):
        yy = lax.rem(y + k, NY)
        p_recv(QUERY, block_at(qall), jnp.maximum(k * NX, 1), (k + 1) * NX)
        at = rows(yy, CHUNK)
        hit_col = to_col(final[pl.ds(16 + yy, 1), :]).astype(jnp.int32)
        top = jnp.full((CHUNK, 1), -jnp.inf, F32)
        positive = jnp.zeros((1, LANES), F32)
        for j in range(tiles):
            here = slice(j * TILE, (j + 1) * TILE)
            scores = 20.0 * lax.dot_general(qall[at, :], bank[here, :], NT, preferred_element_type=F32)
            expo[at, here] = scores
            top = jnp.maximum(top, jnp.max(scores, axis=1, keepdims=True))
            found = jnp.sum(jnp.where(column == hit_col - j * TILE, scores, 0.0), axis=0, keepdims=True)
            for g in range(TILE // LANES):
                positive = positive + found[:, g * LANES:(g + 1) * LANES]
        total = jnp.zeros((CHUNK, 1), F32)
        for j in range(tiles):
            here = slice(j * TILE, (j + 1) * TILE)
            value = jnp.exp(expo[at, here] - top)
            expo[at, here] = value
            total = total + jnp.sum(value, axis=1, keepdims=True)
        base = p * 16
        sp[pl.ds(base + yy, 1), :] = to_row(top)
        sp[pl.ds(base + 8 + yy, 1), :] = to_row(total)
        sp[pl.ds(base + 4, 1), :] += positive
        return carry

    lax.fori_loop(0, NY, score_chunk, 0)

    sp_at = lambda s: sp.at[rows(s, 16), :]
    sz_at = lambda s: sz.at[rows(s, 16), :]
    final[0:8, :] = sp[pl.ds(pl.multiple_of(p * 16, 16), 8), :]

    def combine(ref, n):
        high = ref[0:8, :]
        found = high
        for s in range(1, n):
            part = ref[s * 16:s * 16 + 8, :]
            high = jnp.maximum(high, part)
            found = found + part
        total = jnp.zeros((8, LANES), F32)
        for s in range(n):
            total = total + ref[s * 16 + 8:s * 16 + 16, :] * jnp.exp(ref[s * 16:s * 16 + 8, :] - high)
        return high, found, total

    p_send(STATS, lambda t: sp_at(p), sp_at)
    p_recv(STATS, sp_at)
    high, found, total = combine(sp, PLANE)
    mid = pl.multiple_of(z * 16, 16)
    sz[pl.ds(mid, 8), :] = jnp.where(sub < 4, high, found)
    sz[pl.ds(mid + 8, 8), :] = total
    z_send(STATS, lambda t: sz_at(z), sz_at)
    z_recv(STATS, sz_at)
    high, found, total = combine(sz, NZ)
    lse = high + jnp.log(jnp.where(sub < 4, total, 1.0))
    per_lane = jnp.where(sub < 4, lse, jnp.where(sub == 4, -found, 0.0))
    lossbuf[0:8, :] = jnp.broadcast_to(jnp.sum(per_lane), (8, LANES))
    loss_out = core_copy(1, lossbuf.at[0:8, :], lossbuf.at[8:16, :])
    loss_out.start()
    scale = jnp.exp(final[0:8, :] - lse)
    final[8:16, :] = scale
    final[24:32, :] = high
    top_row = pltpu.roll(final[pl.ds(24 + y, 1), :], lax.rem(LANES - first_lane, LANES), 1)
    top_ref[...] = top_row[:, :OWN]

    def grad_chunk(i, carry):
        k = lax.rem(i + 1, NY)
        yy = lax.rem(y + k, NY)
        at = rows(yy, CHUNK)
        hit_col = to_col(final[pl.ds(16 + yy, 1), :]).astype(jnp.int32)
        scale_col = to_col(final[pl.ds(8 + yy, 1), :])
        for j in range(tiles):
            here = slice(j * TILE, (j + 1) * TILE)
            hits = (column == hit_col - j * TILE).astype(F32)
            coef[:, here] = ((expo[at, here] * scale_col - hits) * (1.0 / QUERIES)).astype(BF16)
        for j in range(E // TILE):
            here = slice(j * TILE, (j + 1) * TILE)
            value = 20.0 * jnp.dot(coef[...], bank[:, here], preferred_element_type=F32)
            gout[at, here] = value.astype(BF16)
        p_each(
            lambda t: p_copy(GRAD, t, block_at(gout)(t), block_at(gin)(p), p).start(),
            jnp.maximum(k * NX, 1), (k + 1) * NX,
        )
        return carry

    lax.fori_loop(0, NY, grad_chunk, 0)
    gin[rows(p, BLOCK), :] = gout[rows(p, BLOCK), :]

    p_recv(STATES, block_at(slab))
    for yy in range(NY):
        turn[...] = jnp.transpose(slab[yy * CHUNK:(yy + 1) * CHUNK, :].astype(F32))
        slab_t[yy] = turn[rows(x, 32), :].astype(BF16)

    acc = gin[rows(p, BLOCK), :].astype(F32)

    def gather(k, acc):
        t = p_peer(k)
        there = block_at(gin)(t)
        p_copy(GRAD, t, there, there, t).wait_recv()
        return acc + gin[rows(t, BLOCK), :].astype(F32)

    acc = lax.fori_loop(1, PLANE, lambda i, a: gather(lax.rem(i + 3, 15) + 1, a), acc)
    for e in range(SPLIT):
        gz_out[pl.ds(e, BLOCK, stride=SPLIT), :] = acc[:, e * LANES:(e + 1) * LANES]
    gz_in[rows(z, BLOCK), :] = gz_out[rows(z, BLOCK), :]
    z_send(GRAD, lambda t: gz_out.at[rows(t, BLOCK), :], lambda s: gz_in.at[rows(s, BLOCK), :])
    z_recv(GRAD, lambda s: gz_in.at[rows(s, BLOCK), :])
    grad = gz_in[0:BLOCK, :]
    for s in range(1, NZ):
        grad = grad + gz_in[s * BLOCK:(s + 1) * BLOCK, :]
    for r in range(OWN):
        one = slice(r * SPLIT, (r + 1) * SPLIT)
        g, u = grad[one, :], unit_s[one, :]
        inner = jnp.sum(jnp.sum(u * g, axis=1, keepdims=True), axis=0, keepdims=True)
        own_gp[one, :] = ((g - u * inner) / radius_s[one, :]).astype(BF16).astype(F32)
    zg[rows(z, BLOCK), :] = own_gp[...]
    zg_at = lambda s: zg.at[rows(s, BLOCK), :]
    z_send(PROJ, lambda t: zg_at(z), zg_at)

    gp = jnp.concatenate(
        [own_gp[pl.ds(e, OWN, stride=SPLIT), :] for e in range(SPLIT)], axis=1
    ).astype(BF16)
    for j in range(H // TILE):
        here = slice(j * TILE, (j + 1) * TILE)
        gs_ref[:, here] = lax.dot_general(gp, w[here, :], NT, preferred_element_type=F32).astype(BF16)

    z_recv(PROJ, zg_at)
    assemble(zg, gpall)
    p_send(PROJ, lambda t: block_at(gpall)(p), block_at(gpall))
    gw_acc[...] = jnp.zeros_like(gw_acc)

    def weight_chunk(k, carry):
        yy = lax.rem(y + k, NY)
        p_recv(PROJ, block_at(gpall), jnp.maximum(k * NX, 1), (k + 1) * NX)
        gw_acc[...] += jnp.dot(slab_t[yy], gpall[rows(yy, CHUNK), :], preferred_element_type=F32)
        return carry

    lax.fori_loop(0, NY, weight_chunk, 0)
    gw_out = core_copy(2, gw_acc.at[rows(1 - c, 16), :], gw_in)
    gw_out.start()
    core_copy(1, lossbuf.at[0:8, :], lossbuf.at[8:16, :]).wait_recv()
    loss_ref[...] = ((lossbuf[0:1, 0:1] + lossbuf[8:9, 0:1]) * (1.0 / QUERIES))
    z_drain(POS, lambda t: posz.at[rows(z, 8), :])
    z_drain(STATES, lambda t: stz_out.at[rows(t, 16), :])
    z_drain(QUERY, lambda t: zq_at(z))
    z_drain(STATS, lambda t: sz_at(z))
    z_drain(GRAD, lambda t: gz_out.at[rows(t, BLOCK), :])
    z_drain(PROJ, lambda t: zg_at(z))
    p_drain(POS, lambda t: posp_at(p))
    p_drain(STATES, st_src)
    p_drain(QUERY, lambda t: block_at(qall)(p))
    p_drain(STATS, lambda t: sp_at(p))
    p_drain(GRAD, lambda t: block_at(gout)(t))
    p_drain(PROJ, lambda t: block_at(gpall)(p))
    bank_out.wait_send()
    loss_out.wait_send()
    gw_out.wait_send()
    gw_out.wait_recv()
    gw_ref[...] = gw_acc[rows(c, 16), :] + gw_in[...]


def local(states, head_weight, bank, positive_index):
    vmem = pltpu.VMEM
    dma = pltpu.SemaphoreType.DMA
    in_vmem = pl.BlockSpec(memory_space=pltpu.VMEM)
    loss, top, grad_states, grad_weight = pl.pallas_call(
        kernel,
        out_shape=(
            jax.ShapeDtypeStruct((1, 1), F32),
            jax.ShapeDtypeStruct((1, OWN), F32),
            jax.ShapeDtypeStruct((OWN, H), BF16),
            jax.ShapeDtypeStruct((16, E), F32),
        ),
        in_specs=[
            in_vmem,
            pl.BlockSpec(memory_space=pl.ANY),
            pl.BlockSpec(memory_space=pl.ANY),
            pl.BlockSpec(memory_space=pltpu.SMEM),
        ],
        out_specs=(in_vmem,) * 4,
        scratch_shapes=[
            vmem((H, E), BF16),
            vmem((2 * BANK, E), BF16),
            vmem((NZ * 8, LANES), jnp.int32),
            vmem((PLANE * 8, LANES), jnp.int32),
            vmem((NZ * 16, LANES), F32),
            vmem((NZ * 16, LANES), F32),
            vmem((NY * BLOCK, LANES), BF16),
            vmem((ROWS, LANES), BF16),
            vmem((NY, 32, CHUNK), BF16),
            vmem((LANES, CHUNK), F32),
            vmem((NZ * BLOCK, LANES), F32),
            vmem((BLOCK, LANES), F32),
            vmem((BLOCK, LANES), F32),
            vmem((ROWS, E), BF16),
            vmem((ROWS, 2 * BANK), F32),
            vmem((CHUNK, 2 * BANK), BF16),
            vmem((PLANE * 16, LANES), F32),
            vmem((NZ * 16, LANES), F32),
            vmem((32, LANES), F32),
            vmem((ROWS, E), BF16),
            vmem((ROWS, E), BF16),
            vmem((NZ * BLOCK, LANES), F32),
            vmem((NZ * BLOCK, LANES), F32),
            vmem((NZ * BLOCK, LANES), F32),
            vmem((BLOCK, LANES), F32),
            vmem((ROWS, E), BF16),
            vmem((32, E), F32),
            vmem((16, E), F32),
            vmem((16, LANES), F32),
            dma((W_PARTS,)), dma,
            dma((3,)), dma((3,)),
            dma((6, NZ)), dma((6, NZ)),
            dma((6, PLANE)), dma((6, PLANE)),
        ],
        compiler_params=pltpu.CompilerParams(
            collective_id=0, has_side_effects=True, vmem_limit_bytes=56 * 2**20
        ),
        name="info_nce",
    )(states, head_weight, bank, positive_index)
    return (loss.reshape(()), top.reshape((OWN,)), grad_states, grad_weight)


def solution(mesh):
    placed = (P("dev", None), P(), P("dev", None), P("dev"))
    return jax.shard_map(
        local,
        mesh=mesh,
        in_specs=placed,
        out_specs=(P(), P("dev"), P("dev", None), P("dev", None)),
        check_vma=False,
    )
```

```python
import jax
import jax.numpy as jnp
from jax import lax
from jax.experimental import pallas as pl
from jax.experimental.pallas import tpu as pltpu
from jax.sharding import PartitionSpec as P

NY, NZ, NX = 4, 8, 4
PLANE = NY * NX
OWN = 4
SETS = 2
PART = OWN // SETS
H, E = 4096, 1024
BANK = 1024
BLOCK = NZ * PART
SET = PLANE * BLOCK
ROWS = SETS * SET
LANES = 128
SPLIT = E // LANES
TILE = 512
W_PARTS = 8
QUERIES = 1024
MESH = pl.DeviceIdType.MESH
NT = (((1,), (1,)), ((), ()))
POS, STATES = 0, 1
QUERY, STATS, GRAD, PROJ = (2, 3), (4, 5), (6, 7), (8, 9)
STAGES = 10
F32, BF16 = jnp.float32, jnp.bfloat16


def kernel(
    states_ref, w_hbm, bank_hbm, pos_ref,
    loss_ref, top_ref, gs_ref, gw_ref,
    w, bank, posz, posp, stz_out, stz_in, stp_out, slab, slab_t, turn,
    zq, zf, unit_s, radius_s, qall, expo, coef, sp, sz, final, gout, gin,
    gz_out, gz_in, zg, own_gp, gpall, gw_acc, gw_in, lossbuf,
    w_sem, bank_sem, cs, cr, zs, zr, ps, pr,
):
    me = lax.axis_index("dev")
    c = lax.rem(me, 2)
    x = lax.rem(me // 2, NX)
    z = lax.rem(me // (2 * NX), NZ)
    y = me // (2 * NX * NZ)
    p = y * NX + x
    chip = me // 2
    partner = chip * 2 + (1 - c)

    def dev(yy, zz, xx):
        return ((yy * NZ + zz) * NX + xx) * 2 + c

    def rows(i, n, base=0):
        return pl.ds(pl.multiple_of(base + i * n, n), n)

    def slots(ref, n, base=0):
        return lambda s: ref.at[rows(s, n, base), :]

    def copy(src, dst, send_sem, recv_sem, target):
        return pltpu.make_async_remote_copy(
            src_ref=src, dst_ref=dst, send_sem=send_sem, recv_sem=recv_sem,
            device_id=(target,), device_id_type=MESH,
        )

    def z_each(body):
        def step(k, carry):
            body(lax.rem(z + k, NZ))
            return carry
        lax.fori_loop(1, NZ, step, 0)

    def p_each(body):
        def step(k, carry):
            body(lax.rem(y + k // NX, NY) * NX + lax.rem(x + lax.rem(k, NX), NX))
            return carry
        lax.fori_loop(1, PLANE, step, 0)

    z_dev = lambda t: dev(y, t, x)
    p_dev = lambda t: dev(t // NX, z, lax.rem(t, NX))

    def z_send(stage, src, dst):
        z_each(lambda t: copy(src(t), dst(z), zs.at[stage], zr.at[stage], z_dev(t)).start())

    def p_send(stage, src, dst):
        p_each(lambda t: copy(src(t), dst(p), ps.at[stage], pr.at[stage], p_dev(t)).start())

    def z_recv(stage, ref, n, base=0):
        part = ref.at[pl.ds(base, (NZ - 1) * n), :]
        copy(part, part, zs.at[stage], zr.at[stage], partner).wait_recv()

    def z_drain(stage, ref, n):
        part = ref.at[pl.ds(0, (NZ - 1) * n), :]
        copy(part, part, zs.at[stage], zr.at[stage], partner).wait_send()

    def p_recv(stage, ref, n, base=0):
        part = ref.at[pl.ds(base, (PLANE - 1) * n), :]
        copy(part, part, ps.at[stage], pr.at[stage], partner).wait_recv()

    def p_drain(stage, ref, n):
        part = ref.at[pl.ds(0, (PLANE - 1) * n), :]
        copy(part, part, ps.at[stage], pr.at[stage], partner).wait_send()

    def w_copy(i):
        part = pl.ds(i * (H // W_PARTS), H // W_PARTS)
        return pltpu.make_async_copy(w_hbm.at[part, :], w.at[part, :], w_sem.at[i])

    for i in range(W_PARTS):
        w_copy(i).start()
    mine = rows(c, BANK)
    other = rows(1 - c, BANK)
    own_bank = pltpu.make_async_copy(bank_hbm, bank.at[mine, :], bank_sem)
    own_bank.start()

    barrier = pltpu.get_barrier_semaphore()

    def greet(target):
        pl.semaphore_signal(barrier, inc=1, device_id=(target,), device_id_type=MESH)

    greet(partner)
    z_each(lambda t: greet(z_dev(t)))
    p_each(lambda t: greet(p_dev(t)))
    lane = lax.broadcasted_iota(jnp.int32, (8, LANES), 1)
    sub = lax.broadcasted_iota(jnp.int32, (8, LANES), 0)
    own_lane = lax.rem(p, 8) * BLOCK + z
    tile = jnp.zeros((8, LANES), jnp.int32)
    for r in range(OWN):
        at_row, at_lane = (r // PART) * 2 + p // 8, own_lane + (r % PART) * NZ
        tile = jnp.where((lane == at_lane) & (sub == at_row), pos_ref[r], tile)
    posz[rows(z, 8), :] = tile
    states_f = states_ref[...].astype(F32)
    for zz in range(NZ):
        for yy in range(NY):
            at = (yy * NZ + zz) * LANES
            stz_out[pl.ds(zz * 16 + yy, OWN, stride=NY), :] = states_f[:, at:at + LANES]
    stz_in[rows(z, 16), :] = stz_out[rows(z, 16), :]
    pl.semaphore_wait(barrier, 1 + (NZ - 1) + (PLANE - 1))

    bank_out = copy(bank_hbm, bank.at[mine, :], cs.at[0], cr.at[0], partner)
    bank_out.start()

    z_send(POS, lambda t: slots(posz, 8)(z), slots(posz, 8))
    z_send(STATES, slots(stz_out, 16), slots(stz_in, 16))

    proj = jnp.zeros((OWN, E), F32)
    for i in range(W_PARTS):
        w_copy(i).wait()
        part = slice(i * (H // W_PARTS), (i + 1) * (H // W_PARTS))
        proj = proj + jnp.dot(states_ref[:, part], w[part, :], preferred_element_type=F32)
    radius = jnp.sqrt(jnp.sum(proj * proj, axis=1, keepdims=True) + 1e-06)
    unit = proj / radius
    radius_b = jnp.broadcast_to(radius, (OWN, LANES))
    for e in range(SPLIT):
        unit_s[pl.ds(e, OWN, stride=SPLIT), :] = unit[:, e * LANES:(e + 1) * LANES]
        radius_s[pl.ds(e, OWN, stride=SPLIT), :] = radius_b
    zq[rows(z, OWN * SPLIT), :] = unit_s[...].astype(BF16)
    zq_at = slots(zq, OWN * SPLIT)
    z_send(QUERY[0], lambda t: zq_at(z), zq_at)

    z_recv(POS, posz, 8)
    tile = jnp.zeros((8, LANES), jnp.int32)
    for s in range(NZ):
        tile = tile + posz[s * 8:(s + 1) * 8, :]
    posp[rows(p, 8), :] = tile
    p_send(POS, lambda t: slots(posp, 8)(p), slots(posp, 8))
    z_recv(STATES, stz_in, 16)
    for yy in range(NY):
        column_slab = [stz_in[pl.ds(r * NY + yy, NZ, stride=16), :] for r in range(OWN)]
        stp_out[yy * 32:(yy + 1) * 32, :] = jnp.concatenate(column_slab, axis=0).astype(BF16)
    slab[rows(p, 32), :] = stp_out[rows(y, 32), :]

    z_recv(QUERY[0], zq, OWN * SPLIT)

    def assemble(base, step, target, s):
        for e in range(SPLIT):
            block = [zf[pl.ds(base + r * SPLIT + e, NZ, stride=step), :] for r in range(PART)]
            target[rows(p, BLOCK, s * SET), e * LANES:(e + 1) * LANES] = jnp.concatenate(block, axis=0).astype(BF16)

    zf[...] = zq[...].astype(F32)
    for s in range(SETS):
        assemble(s * PART * SPLIT, OWN * SPLIT, qall, s)
        at = slots(qall, BLOCK, s * SET)
        p_send(QUERY[s], lambda t: at(p), at)
    p_send(STATES, lambda t: slots(stp_out, 32)(t // NX), slots(slab, 32))
    own_bank.wait()
    copy(bank.at[other, :], bank.at[other, :], cs.at[0], cr.at[0], partner).wait_recv()
    p_recv(POS, posp, 8)
    tile = jnp.zeros((8, LANES), jnp.int32)
    for s in range(PLANE):
        tile = tile + posp[s * 8:(s + 1) * 8, :]
    final[0:8, :] = (tile - chip * (2 * BANK)).astype(F32)

    eye = lax.broadcasted_iota(jnp.int32, (LANES, LANES), 0) == lax.broadcasted_iota(jnp.int32, (LANES, LANES), 1)
    to_row = lambda col: jnp.sum(jnp.where(eye, jnp.broadcast_to(col, (LANES, LANES)), 0.0), axis=0, keepdims=True)
    to_col = lambda row: jnp.sum(jnp.where(eye, jnp.broadcast_to(row, (LANES, LANES)), 0.0), axis=1, keepdims=True)
    tiles = 2 * BANK // TILE
    column = lax.broadcasted_iota(jnp.int32, (LANES, TILE), 1)

    def scores_of(s):
        mine = pl.multiple_of((s * PLANE + p) * 8, 8)
        sp[pl.ds(mine, 8), :] = jnp.zeros((8, LANES), F32)
        p_recv(QUERY[s], qall, BLOCK, s * SET)

        def half(h, carry):
            at = rows(h, LANES, s * SET)
            hit_col = to_col(final[pl.ds(s * 2 + h, 1), :]).astype(jnp.int32)
            top = jnp.full((LANES, 1), -jnp.inf, F32)
            positive = jnp.zeros((1, LANES), F32)
            for j in range(tiles):
                here = slice(j * TILE, (j + 1) * TILE)
                scores = 20.0 * lax.dot_general(qall[at, :], bank[here, :], NT, preferred_element_type=F32)
                expo[at, here] = scores
                top = jnp.maximum(top, jnp.max(scores, axis=1, keepdims=True))
                found = jnp.sum(jnp.where(column == hit_col - j * TILE, scores, 0.0), axis=0, keepdims=True)
                for g in range(TILE // LANES):
                    positive = positive + found[:, g * LANES:(g + 1) * LANES]
            total = jnp.zeros((LANES, 1), F32)
            for j in range(tiles):
                here = slice(j * TILE, (j + 1) * TILE)
                value = jnp.exp(expo[at, here] - top)
                expo[at, here] = value
                total = total + jnp.sum(value, axis=1, keepdims=True)
            sp[pl.ds(mine + h, 1), :] = to_row(top)
            sp[pl.ds(mine + 2 + h, 1), :] = to_row(total)
            sp[pl.ds(mine + 4, 1), :] += positive
            return carry

        lax.fori_loop(0, 2, half, 0)
        final[8 + s * 8:16 + s * 8, :] = sp[pl.ds(mine, 8), :]
        at = slots(sp, 8, s * PLANE * 8)
        p_send(STATS[s], lambda t: at(p), at)

    def combine(ref, base, n):
        high = ref[base:base + 8, :]
        found = high
        for i in range(1, n):
            part = ref[base + i * 8:base + i * 8 + 8, :]
            high = jnp.maximum(high, part)
            found = found + part
        total = jnp.zeros((2, LANES), F32)
        for i in range(n):
            total = total + ref[base + i * 8 + 2:base + i * 8 + 4, :] * jnp.exp(
                ref[base + i * 8:base + i * 8 + 2, :] - high[0:2, :]
            )
        return high[0:2, :], total, found[4:5, :]

    def plane_stats(s):
        p_recv(STATS[s], sp, 8, s * PLANE * 8)
        high, total, found = combine(sp, s * PLANE * 8, PLANE)
        at = pl.multiple_of((s * NZ + z) * 8, 8)
        sz[pl.ds(at, 2), :] = high
        sz[pl.ds(at + 2, 2), :] = total
        sz[pl.ds(at + 4, 4), :] = jnp.concatenate([found, jnp.zeros((3, LANES), F32)], axis=0)
        there = slots(sz, 8, s * NZ * 8)
        z_send(STATS[s], lambda t: there(z), there)

    def all_stats(s):
        z_recv(STATS[s], sz, 8, s * NZ * 8)
        high, total, found = combine(sz, s * NZ * 8, NZ)
        lse = high + jnp.log(total)
        here = 8 + s * 8
        final[here + 2:here + 4, :] = jnp.exp(final[here:here + 2, :] - lse)
        final[here + 4:here + 6, :] = high
        return jnp.sum(lse, axis=0, keepdims=True) - found

    def grad_of(s):
        def half(h, carry):
            at = rows(h, LANES, s * SET)
            hit_col = to_col(final[pl.ds(s * 2 + h, 1), :]).astype(jnp.int32)
            scale_col = to_col(final[pl.ds(8 + s * 8 + 2 + h, 1), :])
            for j in range(tiles):
                here = slice(j * TILE, (j + 1) * TILE)
                hits = (column == hit_col - j * TILE).astype(F32)
                coef[rows(h, LANES), here] = ((expo[at, here] * scale_col - hits) * (1.0 / QUERIES)).astype(BF16)
            return carry

        lax.fori_loop(0, 2, half, 0)
        for j in range(E // TILE):
            here = slice(j * TILE, (j + 1) * TILE)
            value = 20.0 * jnp.dot(coef[...], bank[:, here], preferred_element_type=F32)
            gout[s * SET:(s + 1) * SET, here] = value.astype(BF16)
        p_send(GRAD[s], slots(gout, BLOCK, s * SET), slots(gin, BLOCK, s * SET))
        gin[rows(p, BLOCK, s * SET), :] = gout[rows(p, BLOCK, s * SET), :]

    scores_of(0)
    scores_of(1)
    plane_stats(0)
    plane_stats(1)
    lost = all_stats(0)
    grad_of(0)
    lost = lost + all_stats(1)
    grad_of(1)
    lossbuf[0:8, :] = jnp.broadcast_to(jnp.sum(lost), (8, LANES))
    loss_out = copy(lossbuf.at[0:8, :], lossbuf.at[8:16, :], cs.at[1], cr.at[1], partner)
    loss_out.start()

    top_tile = jnp.zeros((8, LANES), F32)
    for r in range(OWN):
        row = final[pl.ds(8 + (r // PART) * 8 + 4 + p // 8, 1), :]
        mask = lax.broadcasted_iota(jnp.int32, (1, LANES), 1) == own_lane + (r % PART) * NZ
        value = jnp.sum(jnp.where(mask, row, 0.0))
        top_tile = jnp.where(lane == r, value, top_tile)
    top_ref[...] = top_tile
    p_recv(STATES, slab, 32)
    for s in range(SETS):
        part = slab[...].astype(F32).reshape(PLANE, 32, LANES)[:, s * BLOCK:(s + 1) * BLOCK, :].reshape(SET, LANES)
        turn[...] = jnp.transpose(part)
        slab_t[s] = turn[rows(x, 32), :].astype(BF16)

    def line_grad(s):
        p_recv(GRAD[s], gin, BLOCK, s * SET)

        def add(i, acc):
            return acc + gin[rows(i, BLOCK, s * SET), :].astype(F32)

        acc = lax.fori_loop(0, PLANE, add, jnp.zeros((BLOCK, E), F32))
        base = s * NZ * PART * SPLIT
        for e in range(SPLIT):
            for r in range(PART):
                gz_out[pl.ds(base + r * SPLIT + e, NZ, stride=PART * SPLIT), :] = (
                    acc[r * NZ:(r + 1) * NZ, e * LANES:(e + 1) * LANES])
        here, there = slots(gz_out, 16, base), slots(gz_in, 16, base)
        z_send(GRAD[s], here, there)
        gz_in[rows(z, 16, base), :] = gz_out[rows(z, 16, base), :]

    def own_grad(s):
        base = s * NZ * 16
        z_recv(GRAD[s], gz_in, 16, base)
        grad = gz_in[base:base + 16, :]
        for i in range(1, NZ):
            grad = grad + gz_in[base + i * 16:base + (i + 1) * 16, :]
        for r in range(PART):
            one = slice(s * 16 + r * SPLIT, s * 16 + (r + 1) * SPLIT)
            g, u = grad[r * SPLIT:(r + 1) * SPLIT, :], unit_s[one, :]
            inner = jnp.sum(jnp.sum(u * g, axis=1, keepdims=True), axis=0, keepdims=True)
            own_gp[one, :] = (g - u * inner) / radius_s[one, :]
        zg[rows(z, 16, base), :] = own_gp[s * 16:(s + 1) * 16, :].astype(BF16)
        at = slots(zg, 16, base)
        z_send(PROJ[s], lambda t: at(z), at)

    def share_grad(s):
        base = s * NZ * 16
        z_recv(PROJ[s], zg, 16, base)
        zf[0:NZ * 16, :] = zg[base:base + NZ * 16, :].astype(F32)
        assemble(0, 16, gpall, s)
        at = slots(gpall, BLOCK, s * SET)
        p_send(PROJ[s], lambda t: at(p), at)

    line_grad(0)
    line_grad(1)
    own_grad(0)
    own_grad(1)
    share_grad(0)
    share_grad(1)

    gp = jnp.concatenate(
        [own_gp[pl.ds(e, OWN, stride=SPLIT), :] for e in range(SPLIT)], axis=1
    ).astype(BF16)
    for j in range(H // TILE):
        here = slice(j * TILE, (j + 1) * TILE)
        gs_ref[:, here] = lax.dot_general(gp, w[here, :], NT, preferred_element_type=F32).astype(BF16)

    z_drain(POS, posz, 8)
    z_drain(STATES, stz_out, 16)
    z_drain(QUERY[0], zq, OWN * SPLIT)
    p_drain(POS, posp, 8)
    p_drain(STATES, slab, 32)
    for s in range(SETS):
        z_drain(STATS[s], sz, 8)
        z_drain(GRAD[s], gz_out, 16)
        z_drain(PROJ[s], zg, 16)
        p_drain(QUERY[s], qall, BLOCK)
        p_drain(STATS[s], sp, 8)
        p_drain(GRAD[s], gout, BLOCK)
    bank_out.wait_send()
    loss_out.wait()
    loss_ref[...] = (lossbuf[0:8, :] + lossbuf[8:16, :]) * (1.0 / QUERIES)

    p_recv(PROJ[0], gpall, BLOCK, 0)
    gw_acc[...] = jnp.dot(slab_t[0], gpall[0:SET, :], preferred_element_type=F32)
    p_recv(PROJ[1], gpall, BLOCK, SET)
    gw_acc[...] += jnp.dot(slab_t[1], gpall[SET:ROWS, :], preferred_element_type=F32)
    gw_out = copy(gw_acc.at[rows(1 - c, 16), :], gw_in, cs.at[2], cr.at[2], partner)
    gw_out.start()
    p_drain(PROJ[0], gpall, BLOCK)
    p_drain(PROJ[1], gpall, BLOCK)
    gw_out.wait()
    gw_ref[...] = gw_acc[rows(c, 16), :] + gw_in[...]


def hand_over(loss_in, top_in, gs_in, gw_in, loss_ref, top_ref, gs_ref, gw_ref):
    loss_ref[...] = loss_in[0:1, 0:1]
    top_ref[...] = top_in[0:1, 0:OWN]
    gs_ref[...] = gs_in[...]
    gw_ref[...] = gw_in[...]


def local(states, head_weight, bank, positive_index):
    vmem = pltpu.VMEM
    dma = pltpu.SemaphoreType.DMA
    in_vmem = pl.BlockSpec(memory_space=pltpu.VMEM)
    grads = (jax.ShapeDtypeStruct((OWN, H), BF16), jax.ShapeDtypeStruct((16, E), F32))
    parts = pl.pallas_call(
        kernel,
        out_shape=(jax.ShapeDtypeStruct((8, LANES), F32),) * 2 + grads,
        in_specs=[
            in_vmem,
            pl.BlockSpec(memory_space=pl.ANY),
            pl.BlockSpec(memory_space=pl.ANY),
            pl.BlockSpec(memory_space=pltpu.SMEM),
        ],
        out_specs=(in_vmem,) * 4,
        scratch_shapes=[
            vmem((H, E), BF16),
            vmem((2 * BANK, E), BF16),
            vmem((NZ * 8, LANES), jnp.int32),
            vmem((PLANE * 8, LANES), jnp.int32),
            vmem((NZ * 16, LANES), F32),
            vmem((NZ * 16, LANES), F32),
            vmem((NY * 32, LANES), BF16),
            vmem((ROWS, LANES), BF16),
            vmem((SETS, 32, SET), BF16),
            vmem((LANES, SET), F32),
            vmem((NZ * OWN * SPLIT, LANES), BF16),
            vmem((NZ * OWN * SPLIT, LANES), F32),
            vmem((OWN * SPLIT, LANES), F32),
            vmem((OWN * SPLIT, LANES), F32),
            vmem((ROWS, E), BF16),
            vmem((ROWS, 2 * BANK), F32),
            vmem((SET, 2 * BANK), BF16),
            vmem((SETS * PLANE * 8, LANES), F32),
            vmem((SETS * NZ * 8, LANES), F32),
            vmem((24, LANES), F32),
            vmem((ROWS, E), BF16),
            vmem((ROWS, E), BF16),
            vmem((SETS * NZ * 16, LANES), F32),
            vmem((SETS * NZ * 16, LANES), F32),
            vmem((SETS * NZ * 16, LANES), BF16),
            vmem((OWN * SPLIT, LANES), F32),
            vmem((ROWS, E), BF16),
            vmem((32, E), F32),
            vmem((16, E), F32),
            vmem((16, LANES), F32),
            dma((W_PARTS,)), dma,
            dma((3,)), dma((3,)),
            dma((STAGES,)), dma((STAGES,)),
            dma((STAGES,)), dma((STAGES,)),
        ],
        compiler_params=pltpu.CompilerParams(
            collective_id=0, has_side_effects=True, vmem_limit_bytes=56 * 2**20
        ),
        name="info_nce",
    )(states, head_weight, bank, positive_index)
    loss, top, grad_states, grad_weight = pl.pallas_call(
        hand_over,
        out_shape=(jax.ShapeDtypeStruct((1, 1), F32), jax.ShapeDtypeStruct((1, OWN), F32)) + grads,
        in_specs=[in_vmem] * 4,
        out_specs=(in_vmem,) * 4,
        name="hand_over",
    )(*parts)
    return (loss.reshape(()), top.reshape((OWN,)), grad_states, grad_weight)


def solution(mesh):
    placed = (P("dev", None), P(), P("dev", None), P("dev"))
    return jax.shard_map(
        local,
        mesh=mesh,
        in_specs=placed,
        out_specs=(P(), P("dev"), P("dev", None), P("dev", None)),
        check_vma=False,
    )
```

```python
import jax
import jax.numpy as jnp
from jax import lax
from jax.experimental import pallas as pl
from jax.experimental.pallas import tpu as pltpu
from jax.sharding import PartitionSpec as P

NY, NZ, NX = 4, 8, 4
PLANE = NY * NX
OWN = 4
SETS = 2
PART = OWN // SETS
H, E = 4096, 1024
BANK = 1024
BLOCK = NZ * PART
SET = PLANE * BLOCK
ROWS = SETS * SET
LANES = 128
SPLIT = E // LANES
TILE = 512
W_PARTS = 8
QUERIES = 1024
MESH = pl.DeviceIdType.MESH
NT = (((1,), (1,)), ((), ()))
POS, STATES = 0, 1
QUERY, STATS, GRAD, PROJ = (2, 3), (4, 5), (6, 7), (8, 9)
LEFT_X, LEFT_Y, RIGHT_Y, RIGHT_X = (2, 3), (10, 11), (12, 13), (14, 15)
STAGES = 16
HALF = E // 2
F32, BF16 = jnp.float32, jnp.bfloat16


def kernel(
    states_ref, w_hbm, bank_hbm, pos_ref,
    loss_ref, top_ref, gs_ref, gw_ref,
    w, bank, posz, posp, stz_out, stz_in, stp_out, slab, slab_t, turn,
    zq, zf, unit_s, radius_s, qleft, qright, expo, coef, sp, sz, final, gout, gin,
    gz_out, gz_in, zg, own_gp, gpall, gw_acc, gw_in, lossbuf,
    w_sem, bank_sem, cs, cr, zs, zr, ps, pr,
):
    me = lax.axis_index("dev")
    c = lax.rem(me, 2)
    x = lax.rem(me // 2, NX)
    z = lax.rem(me // (2 * NX), NZ)
    y = me // (2 * NX * NZ)
    p = y * NX + x
    chip = me // 2
    partner = chip * 2 + (1 - c)

    def dev(yy, zz, xx):
        return ((yy * NZ + zz) * NX + xx) * 2 + c

    def rows(i, n, base=0):
        return pl.ds(pl.multiple_of(base + i * n, n), n)

    def slots(ref, n, base=0):
        return lambda s: ref.at[rows(s, n, base), :]

    def copy(src, dst, send_sem, recv_sem, target):
        return pltpu.make_async_remote_copy(
            src_ref=src, dst_ref=dst, send_sem=send_sem, recv_sem=recv_sem,
            device_id=(target,), device_id_type=MESH,
        )

    def z_each(body):
        def step(k, carry):
            body(lax.rem(z + 4 + (k // 2 + k % 2) * (1 - 2 * (k % 2)), NZ))
            return carry
        lax.fori_loop(0, NZ - 1, step, 0)

    def away(k):
        return 2 * (1 - k % 2) + (k % 2 + k // 2) % 2

    def p_each(body):
        def step(k, carry):
            body(lax.rem(y + away(k // NX), NY) * NX + lax.rem(x + away(k % NX), NX))
            return carry
        lax.fori_loop(0, PLANE - 1, step, 0)

    z_dev = lambda t: dev(y, t, x)
    p_dev = lambda t: dev(t // NX, z, lax.rem(t, NX))

    def z_send(stage, src, dst):
        z_each(lambda t: copy(src(t), dst(z), zs.at[stage], zr.at[stage], z_dev(t)).start())

    def p_send(stage, src, dst):
        p_each(lambda t: copy(src(t), dst(p), ps.at[stage], pr.at[stage], p_dev(t)).start())

    def z_recv(stage, ref, n, base=0):
        part = ref.at[pl.ds(base, (NZ - 1) * n), :]
        copy(part, part, zs.at[stage], zr.at[stage], partner).wait_recv()

    def z_drain(stage, ref, n):
        part = ref.at[pl.ds(0, (NZ - 1) * n), :]
        copy(part, part, zs.at[stage], zr.at[stage], partner).wait_send()

    def p_recv(stage, ref, n, base=0):
        part = ref.at[pl.ds(base, (PLANE - 1) * n), :]
        copy(part, part, ps.at[stage], pr.at[stage], partner).wait_recv()

    def p_drain(stage, ref, n):
        part = ref.at[pl.ds(0, (PLANE - 1) * n), :]
        copy(part, part, ps.at[stage], pr.at[stage], partner).wait_send()

    def w_copy(i):
        part = pl.ds(i * (H // W_PARTS), H // W_PARTS)
        return pltpu.make_async_copy(w_hbm.at[part, :], w.at[part, :], w_sem.at[i])

    for i in range(W_PARTS):
        w_copy(i).start()
    mine = rows(c, BANK)
    other = rows(1 - c, BANK)
    own_bank = pltpu.make_async_copy(bank_hbm, bank.at[mine, :], bank_sem)

    barrier = pltpu.get_barrier_semaphore()

    def greet(target):
        pl.semaphore_signal(barrier, inc=1, device_id=(target,), device_id_type=MESH)

    greet(partner)
    z_each(lambda t: greet(z_dev(t)))
    p_each(lambda t: greet(p_dev(t)))
    lane = lax.broadcasted_iota(jnp.int32, (8, LANES), 1)
    sub = lax.broadcasted_iota(jnp.int32, (8, LANES), 0)
    own_lane = lax.rem(p, 8) * BLOCK + z
    tile = jnp.zeros((8, LANES), jnp.int32)
    for r in range(OWN):
        at_row, at_lane = (r // PART) * 2 + p // 8, own_lane + (r % PART) * NZ
        tile = jnp.where((lane == at_lane) & (sub == at_row), pos_ref[r], tile)
    posz[rows(z, 8), :] = tile
    states_f = states_ref[...].astype(F32)
    for zz in range(NZ):
        for yy in range(NY):
            at = (yy * NZ + zz) * LANES
            stz_out[pl.ds(zz * 16 + yy, OWN, stride=NY), :] = states_f[:, at:at + LANES]
    stz_in[rows(z, 16), :] = stz_out[rows(z, 16), :]
    pl.semaphore_wait(barrier, 1 + (NZ - 1) + (PLANE - 1))

    bank_out = copy(bank_hbm, bank.at[mine, :], cs.at[0], cr.at[0], partner)
    z_send(POS, lambda t: slots(posz, 8)(z), slots(posz, 8))
    z_send(STATES, slots(stz_out, 16), slots(stz_in, 16))

    bank_out.start()
    own_bank.start()

    proj = jnp.zeros((OWN, E), F32)
    for i in range(W_PARTS):
        w_copy(i).wait()
        part = slice(i * (H // W_PARTS), (i + 1) * (H // W_PARTS))
        proj = proj + jnp.dot(states_ref[:, part], w[part, :], preferred_element_type=F32)
    radius = jnp.sqrt(jnp.sum(proj * proj, axis=1, keepdims=True) + 1e-06)
    unit = proj / radius
    radius_b = jnp.broadcast_to(radius, (OWN, LANES))
    for e in range(SPLIT):
        unit_s[pl.ds(e, OWN, stride=SPLIT), :] = unit[:, e * LANES:(e + 1) * LANES]
        radius_s[pl.ds(e, OWN, stride=SPLIT), :] = radius_b
    zq[rows(z, OWN * SPLIT), :] = unit_s[...].astype(BF16)
    zq_at = slots(zq, OWN * SPLIT)
    z_send(QUERY[0], lambda t: zq_at(z), zq_at)

    z_recv(POS, posz, 8)
    tile = jnp.zeros((8, LANES), jnp.int32)
    for s in range(NZ):
        tile = tile + posz[s * 8:(s + 1) * 8, :]
    posp[rows(p, 8), :] = tile
    p_send(POS, lambda t: slots(posp, 8)(p), slots(posp, 8))
    z_recv(STATES, stz_in, 16)
    for yy in range(NY):
        column_slab = [stz_in[pl.ds(r * NY + yy, NZ, stride=16), :] for r in range(OWN)]
        stp_out[yy * 32:(yy + 1) * 32, :] = jnp.concatenate(column_slab, axis=0).astype(BF16)
    slab[rows(p, 32), :] = stp_out[rows(y, 32), :]

    z_recv(QUERY[0], zq, OWN * SPLIT)

    def gathered(base, step, e):
        block = [zf[pl.ds(base + r * SPLIT + e, NZ, stride=step), :] for r in range(PART)]
        return jnp.concatenate(block, axis=0).astype(BF16)

    x_peers = [lax.rem(x + k, NX) for k in (2, 1, 3)]
    y_peers = [lax.rem(y + k, NY) for k in (2, 1, 3)]

    def p_start(stage, ref, target):
        copy(ref, ref, ps.at[stage], pr.at[stage], target).start()

    zf[...] = zq[...].astype(F32)
    for s in range(SETS):
        for e in range(SPLIT // 2):
            here = slice(e * LANES, (e + 1) * LANES)
            qleft[s * NY + y, x, :, here] = gathered(s * PART * SPLIT, OWN * SPLIT, e)
            qright[s * NY + y, x, :, here] = gathered(s * PART * SPLIT, OWN * SPLIT, SPLIT // 2 + e)
        for i in range(3):
            p_start(LEFT_X[s], qleft.at[s * NY + y, x], dev(y, z, x_peers[i]))
            p_start(RIGHT_Y[s], qright.at[s * NY + y, x], dev(y_peers[i], z, x))

    def q_wait(stage, ref):
        return copy(ref, ref, ps.at[stage], pr.at[stage], partner)

    three_blocks = lambda ref, s: ref.at[s * NY, pl.ds(0, 3)]
    three_lines = lambda ref, s: ref.at[pl.ds(s * NY, 3)]
    for s in range(SETS):
        q_wait(LEFT_X[s], three_blocks(qleft, s)).wait_recv()
        for i in range(3):
            p_start(LEFT_Y[s], qleft.at[s * NY + y], dev(y_peers[i], z, x))
        q_wait(RIGHT_Y[s], three_blocks(qright, s)).wait_recv()
        for i in range(3):
            p_start(RIGHT_X[s], qright.at[pl.ds(s * NY, NY), x], dev(y, z, x_peers[i]))
    p_send(STATES, lambda t: slots(stp_out, 32)(t // NX), slots(slab, 32))
    own_bank.wait()
    copy(bank.at[other, :], bank.at[other, :], cs.at[0], cr.at[0], partner).wait_recv()
    p_recv(POS, posp, 8)
    tile = jnp.zeros((8, LANES), jnp.int32)
    for s in range(PLANE):
        tile = tile + posp[s * 8:(s + 1) * 8, :]
    final[0:8, :] = (tile - chip * (2 * BANK)).astype(F32)

    eye = lax.broadcasted_iota(jnp.int32, (LANES, LANES), 0) == lax.broadcasted_iota(jnp.int32, (LANES, LANES), 1)
    to_row = lambda col: jnp.sum(jnp.where(eye, jnp.broadcast_to(col, (LANES, LANES)), 0.0), axis=0, keepdims=True)
    to_col = lambda row: jnp.sum(jnp.where(eye, jnp.broadcast_to(row, (LANES, LANES)), 0.0), axis=1, keepdims=True)
    tiles = 2 * BANK // TILE
    column = lax.broadcasted_iota(jnp.int32, (SET, LANES), 1)
    two_cols = lambda base: jnp.concatenate([to_col(final[base + h:base + h + 1, :]) for h in range(2)], axis=0)
    hits_of = lambda s: two_cols(s * 2).astype(jnp.int32)

    def scores_of(s):
        mine = pl.multiple_of((s * PLANE + p) * 8, 8)
        sp[pl.ds(mine, 8), :] = jnp.zeros((8, LANES), F32)
        q_wait(LEFT_Y[s], three_lines(qleft, s)).wait_recv()
        q_wait(RIGHT_X[s], three_lines(qright, s)).wait_recv()
        at = slice(s * SET, (s + 1) * SET)
        left = qleft[s * NY:(s + 1) * NY].reshape(SET, HALF)
        right = qright[s * NY:(s + 1) * NY].reshape(SET, HALF)
        hit_col = hits_of(s)
        groups = [slice(g * LANES, (g + 1) * LANES) for g in range(TILE // LANES)]
        top, positive = None, jnp.zeros((SET, LANES), F32)
        for j in range(tiles):
            here = slice(j * TILE, (j + 1) * TILE)
            scores = 20.0 * (
                lax.dot_general(left, bank[here, 0:HALF], NT, preferred_element_type=F32)
                + lax.dot_general(right, bank[here, HALF:E], NT, preferred_element_type=F32)
            )
            expo[at, here] = scores
            for g in groups:
                part = scores[:, g]
                top = part if top is None else jnp.maximum(top, part)
                positive = positive + jnp.where(column == hit_col - (j * TILE + g.start), part, 0.0)
        top = jnp.max(top, axis=1, keepdims=True)
        total = jnp.zeros((SET, LANES), F32)
        for j in range(tiles):
            here = slice(j * TILE, (j + 1) * TILE)
            value = jnp.exp(expo[at, here] - top)
            expo[at, here] = value
            for g in groups:
                total = total + value[:, g]
        total = jnp.sum(total, axis=1, keepdims=True)
        for h in range(2):
            half = slice(h * LANES, (h + 1) * LANES)
            sp[pl.ds(mine + h, 1), :] = to_row(top[half, :])
            sp[pl.ds(mine + 2 + h, 1), :] = to_row(total[half, :])
        sp[pl.ds(mine + 4, 1), :] = jnp.sum(positive, axis=0, keepdims=True)
        final[8 + s * 8:16 + s * 8, :] = sp[pl.ds(mine, 8), :]
        at = slots(sp, 8, s * PLANE * 8)
        p_send(STATS[s], lambda t: at(p), at)

    def combine(ref, base, n):
        high = ref[base:base + 8, :]
        found = high
        for i in range(1, n):
            part = ref[base + i * 8:base + i * 8 + 8, :]
            high = jnp.maximum(high, part)
            found = found + part
        total = jnp.zeros((2, LANES), F32)
        for i in range(n):
            total = total + ref[base + i * 8 + 2:base + i * 8 + 4, :] * jnp.exp(
                ref[base + i * 8:base + i * 8 + 2, :] - high[0:2, :]
            )
        return high[0:2, :], total, found[4:5, :]

    def plane_stats(s):
        p_recv(STATS[s], sp, 8, s * PLANE * 8)
        high, total, found = combine(sp, s * PLANE * 8, PLANE)
        at = pl.multiple_of((s * NZ + z) * 8, 8)
        sz[pl.ds(at, 2), :] = high
        sz[pl.ds(at + 2, 2), :] = total
        sz[pl.ds(at + 4, 4), :] = jnp.concatenate([found, jnp.zeros((3, LANES), F32)], axis=0)
        there = slots(sz, 8, s * NZ * 8)
        z_send(STATS[s], lambda t: there(z), there)

    def all_stats(s):
        z_recv(STATS[s], sz, 8, s * NZ * 8)
        high, total, found = combine(sz, s * NZ * 8, NZ)
        lse = high + jnp.log(total)
        here = 8 + s * 8
        final[here + 2:here + 4, :] = jnp.exp(final[here:here + 2, :] - lse)
        final[here + 4:here + 6, :] = high
        return jnp.sum(lse, axis=0, keepdims=True) - found

    def grad_of(s):
        at = slice(s * SET, (s + 1) * SET)
        hit_col = hits_of(s)
        scale_col = two_cols(8 + s * 8 + 2)
        for j in range(2 * BANK // LANES):
            here = slice(j * LANES, (j + 1) * LANES)
            hits = (column == hit_col - j * LANES).astype(F32)
            coef[:, here] = ((expo[at, here] * scale_col - hits) * (1.0 / QUERIES)).astype(BF16)
        for j in range(E // TILE):
            here = slice(j * TILE, (j + 1) * TILE)
            value = 20.0 * jnp.dot(coef[...], bank[:, here], preferred_element_type=F32)
            gout[s * SET:(s + 1) * SET, here] = value.astype(BF16)
        p_send(GRAD[s], slots(gout, BLOCK, s * SET), slots(gin, BLOCK, s * SET))
        gin[rows(p, BLOCK, s * SET), :] = gout[rows(p, BLOCK, s * SET), :]

    scores_of(0)
    scores_of(1)
    plane_stats(0)
    plane_stats(1)
    lost = all_stats(0)
    grad_of(0)
    lost = lost + all_stats(1)
    grad_of(1)
    lossbuf[0:8, :] = jnp.broadcast_to(jnp.sum(lost), (8, LANES))
    loss_out = copy(lossbuf.at[0:8, :], lossbuf.at[8:16, :], cs.at[1], cr.at[1], partner)
    loss_out.start()

    top_tile = jnp.zeros((8, LANES), F32)
    for r in range(OWN):
        row = final[pl.ds(8 + (r // PART) * 8 + 4 + p // 8, 1), :]
        mask = lax.broadcasted_iota(jnp.int32, (1, LANES), 1) == own_lane + (r % PART) * NZ
        value = jnp.sum(jnp.where(mask, row, 0.0))
        top_tile = jnp.where(lane == r, value, top_tile)
    top_ref[...] = top_tile
    p_recv(STATES, slab, 32)
    for s in range(SETS):
        part = slab[...].astype(F32).reshape(PLANE, 32, LANES)[:, s * BLOCK:(s + 1) * BLOCK, :].reshape(SET, LANES)
        turn[...] = jnp.transpose(part)
        slab_t[s] = turn[rows(x, 32), :].astype(BF16)

    def line_grad(s):
        p_recv(GRAD[s], gin, BLOCK, s * SET)

        def add(i, acc):
            return acc + gin[rows(i, BLOCK, s * SET), :].astype(F32)

        acc = lax.fori_loop(0, PLANE, add, jnp.zeros((BLOCK, E), F32))
        base = s * NZ * PART * SPLIT
        for e in range(SPLIT):
            for r in range(PART):
                gz_out[pl.ds(base + r * SPLIT + e, NZ, stride=PART * SPLIT), :] = (
                    acc[r * NZ:(r + 1) * NZ, e * LANES:(e + 1) * LANES])
        here, there = slots(gz_out, 16, base), slots(gz_in, 16, base)
        z_send(GRAD[s], here, there)
        gz_in[rows(z, 16, base), :] = gz_out[rows(z, 16, base), :]

    def own_grad(s):
        base = s * NZ * 16
        z_recv(GRAD[s], gz_in, 16, base)
        grad = gz_in[base:base + 16, :]
        for i in range(1, NZ):
            grad = grad + gz_in[base + i * 16:base + (i + 1) * 16, :]
        for r in range(PART):
            one = slice(s * 16 + r * SPLIT, s * 16 + (r + 1) * SPLIT)
            g, u = grad[r * SPLIT:(r + 1) * SPLIT, :], unit_s[one, :]
            inner = jnp.sum(jnp.sum(u * g, axis=1, keepdims=True), axis=0, keepdims=True)
            own_gp[one, :] = (g - u * inner) / radius_s[one, :]
        zg[rows(z, 16, base), :] = own_gp[s * 16:(s + 1) * 16, :].astype(BF16)
        at = slots(zg, 16, base)
        z_send(PROJ[s], lambda t: at(z), at)

    def share_grad(s):
        base = s * NZ * 16
        z_recv(PROJ[s], zg, 16, base)
        zf[0:NZ * 16, :] = zg[base:base + NZ * 16, :].astype(F32)
        for e in range(SPLIT):
            gpall[rows(p, BLOCK, s * SET), e * LANES:(e + 1) * LANES] = gathered(0, 16, e)
        at = slots(gpall, BLOCK, s * SET)
        p_send(PROJ[s], lambda t: at(p), at)

    line_grad(0)
    line_grad(1)
    own_grad(0)
    own_grad(1)
    share_grad(0)
    share_grad(1)

    gp = jnp.concatenate(
        [own_gp[pl.ds(e, OWN, stride=SPLIT), :] for e in range(SPLIT)], axis=1
    ).astype(BF16)
    for j in range(H // TILE):
        here = slice(j * TILE, (j + 1) * TILE)
        gs_ref[:, here] = lax.dot_general(gp, w[here, :], NT, preferred_element_type=F32).astype(BF16)

    z_drain(POS, posz, 8)
    z_drain(STATES, stz_out, 16)
    z_drain(QUERY[0], zq, OWN * SPLIT)
    p_drain(POS, posp, 8)
    p_drain(STATES, slab, 32)
    for s in range(SETS):
        z_drain(STATS[s], sz, 8)
        z_drain(GRAD[s], gz_out, 16)
        z_drain(PROJ[s], zg, 16)
        q_wait(LEFT_X[s], three_blocks(qleft, s)).wait_send()
        q_wait(LEFT_Y[s], three_lines(qleft, s)).wait_send()
        q_wait(RIGHT_Y[s], three_blocks(qright, s)).wait_send()
        q_wait(RIGHT_X[s], three_lines(qright, s)).wait_send()
        p_drain(STATS[s], sp, 8)
        p_drain(GRAD[s], gout, BLOCK)
    bank_out.wait_send()
    loss_out.wait()
    loss_ref[...] = (lossbuf[0:8, :] + lossbuf[8:16, :]) * (1.0 / QUERIES)

    p_recv(PROJ[0], gpall, BLOCK, 0)
    gw_acc[...] = jnp.dot(slab_t[0], gpall[0:SET, :], preferred_element_type=F32)
    p_recv(PROJ[1], gpall, BLOCK, SET)
    gw_acc[...] += jnp.dot(slab_t[1], gpall[SET:ROWS, :], preferred_element_type=F32)
    gw_out = copy(gw_acc.at[rows(1 - c, 16), :], gw_in, cs.at[2], cr.at[2], partner)
    gw_out.start()
    p_drain(PROJ[0], gpall, BLOCK)
    p_drain(PROJ[1], gpall, BLOCK)
    gw_out.wait()
    gw_ref[...] = gw_acc[rows(c, 16), :] + gw_in[...]


def hand_over(loss_in, top_in, gs_in, gw_in, loss_ref, top_ref, gs_ref, gw_ref):
    loss_ref[...] = loss_in[0:1, 0:1]
    top_ref[...] = top_in[0:1, 0:OWN]
    gs_ref[...] = gs_in[...]
    gw_ref[...] = gw_in[...]


def local(states, head_weight, bank, positive_index):
    vmem = pltpu.VMEM
    dma = pltpu.SemaphoreType.DMA
    in_vmem = pl.BlockSpec(memory_space=pltpu.VMEM)
    grads = (jax.ShapeDtypeStruct((OWN, H), BF16), jax.ShapeDtypeStruct((16, E), F32))
    parts = pl.pallas_call(
        kernel,
        out_shape=(jax.ShapeDtypeStruct((8, LANES), F32),) * 2 + grads,
        in_specs=[
            in_vmem,
            pl.BlockSpec(memory_space=pl.ANY),
            pl.BlockSpec(memory_space=pl.ANY),
            pl.BlockSpec(memory_space=pltpu.SMEM),
        ],
        out_specs=(in_vmem,) * 4,
        scratch_shapes=[
            vmem((H, E), BF16),
            vmem((2 * BANK, E), BF16),
            vmem((NZ * 8, LANES), jnp.int32),
            vmem((PLANE * 8, LANES), jnp.int32),
            vmem((NZ * 16, LANES), F32),
            vmem((NZ * 16, LANES), F32),
            vmem((NY * 32, LANES), BF16),
            vmem((ROWS, LANES), BF16),
            vmem((SETS, 32, SET), BF16),
            vmem((LANES, SET), F32),
            vmem((NZ * OWN * SPLIT, LANES), BF16),
            vmem((NZ * OWN * SPLIT, LANES), F32),
            vmem((OWN * SPLIT, LANES), F32),
            vmem((OWN * SPLIT, LANES), F32),
            vmem((SETS * NY, NX, BLOCK, HALF), BF16),
            vmem((SETS * NY, NX, BLOCK, HALF), BF16),
            vmem((ROWS, 2 * BANK), F32),
            vmem((SET, 2 * BANK), BF16),
            vmem((SETS * PLANE * 8, LANES), F32),
            vmem((SETS * NZ * 8, LANES), F32),
            vmem((24, LANES), F32),
            vmem((ROWS, E), BF16),
            vmem((ROWS, E), BF16),
            vmem((SETS * NZ * 16, LANES), F32),
            vmem((SETS * NZ * 16, LANES), F32),
            vmem((SETS * NZ * 16, LANES), BF16),
            vmem((OWN * SPLIT, LANES), F32),
            vmem((ROWS, E), BF16),
            vmem((32, E), F32),
            vmem((16, E), F32),
            vmem((16, LANES), F32),
            dma((W_PARTS,)), dma,
            dma((3,)), dma((3,)),
            dma((STAGES,)), dma((STAGES,)),
            dma((STAGES,)), dma((STAGES,)),
        ],
        compiler_params=pltpu.CompilerParams(
            collective_id=0, has_side_effects=True, vmem_limit_bytes=56 * 2**20
        ),
        name="info_nce",
    )(states, head_weight, bank, positive_index)
    loss, top, grad_states, grad_weight = pl.pallas_call(
        hand_over,
        out_shape=(jax.ShapeDtypeStruct((1, 1), F32), jax.ShapeDtypeStruct((1, OWN), F32)) + grads,
        in_specs=[in_vmem] * 4,
        out_specs=(in_vmem,) * 4,
        name="hand_over",
    )(*parts)
    return (loss.reshape(()), top.reshape((OWN,)), grad_states, grad_weight)


def solution(mesh):
    placed = (P("dev", None), P(), P("dev", None), P("dev"))
    return jax.shard_map(
        local,
        mesh=mesh,
        in_specs=placed,
        out_specs=(P(), P("dev"), P("dev", None), P("dev", None)),
        check_vma=False,
    )
```

```python
import jax
import jax.numpy as jnp
from jax import lax
from jax.experimental import pallas as pl
from jax.experimental.pallas import tpu as pltpu
from jax.sharding import PartitionSpec as P

NY, NZ, NX = 4, 8, 4
PLANE = NY * NX
OWN = 4
SETS = 2
PART = OWN // SETS
H, E = 4096, 1024
BANK = 1024
BLOCK = NZ * PART
SET = PLANE * BLOCK
ROWS = SETS * SET
LANES = 128
SPLIT = E // LANES
TILE = 512
W_PARTS = 8
QUERIES = 1024
MESH = pl.DeviceIdType.MESH
NT = (((1,), (1,)), ((), ()))
POS, STATES = 0, 1
QUERY, STATS, GRAD, PROJ = (2, 3), (4, 5), (6, 7), (8, 9)
LEFT_X, LEFT_Y, RIGHT_Y, RIGHT_X = (2, 3), (10, 11), (12, 13), (14, 15)
UNIT, TURNED, OWNERS, WEIGHT = 3, 10, 8, 9
STAGES = 16
HALF = E // 2
F32, BF16 = jnp.float32, jnp.bfloat16


def kernel(
    states_ref, w_hbm, bank_hbm, pos_ref,
    loss_ref, top_ref, gs_ref, gw_ref,
    w, bank, posz, posp, stz_out, stz_in, stp_out, slab, turned, turn,
    zq, zf, unit_s, uz_out, uz_in, qleft, qright, expo, coef, pre, chosen, sp, sz, final, gout, gin,
    gz_out, gz_in, gs_out, gs_in, gpall, gw_all, gw_in, gw_out, gw_parts, lossbuf,
    w_sem, bank_sem, cs, cr, zs, zr, ps, pr,
):
    me = lax.axis_index("dev")
    c = lax.rem(me, 2)
    x = lax.rem(me // 2, NX)
    z = lax.rem(me // (2 * NX), NZ)
    y = me // (2 * NX * NZ)
    p = y * NX + x
    chip = me // 2
    partner = chip * 2 + (1 - c)

    def dev(yy, zz, xx):
        return ((yy * NZ + zz) * NX + xx) * 2 + c

    def rows(i, n, base=0):
        return pl.ds(pl.multiple_of(base + i * n, n), n)

    def slots(ref, n, base=0):
        return lambda s: ref.at[rows(s, n, base), :]

    def copy(src, dst, send_sem, recv_sem, target):
        return pltpu.make_async_remote_copy(
            src_ref=src, dst_ref=dst, send_sem=send_sem, recv_sem=recv_sem,
            device_id=(target,), device_id_type=MESH,
        )

    def z_each(body):
        def step(k, carry):
            body(lax.rem(z + 4 + (k // 2 + k % 2) * (1 - 2 * (k % 2)), NZ))
            return carry
        lax.fori_loop(0, NZ - 1, step, 0)

    def away(k):
        return 2 * (1 - k % 2) + (k % 2 + k // 2) % 2

    def p_each(body):
        def step(k, carry):
            body(lax.rem(y + away(k // NX), NY) * NX + lax.rem(x + away(k % NX), NX))
            return carry
        lax.fori_loop(0, PLANE - 1, step, 0)

    z_dev = lambda t: dev(y, t, x)
    p_dev = lambda t: dev(t // NX, z, lax.rem(t, NX))

    def z_send(stage, src, dst):
        z_each(lambda t: copy(src(t), dst(z), zs.at[stage], zr.at[stage], z_dev(t)).start())

    def p_send(stage, src, dst):
        p_each(lambda t: copy(src(t), dst(p), ps.at[stage], pr.at[stage], p_dev(t)).start())

    def z_recv(stage, ref, n, base=0):
        part = ref.at[pl.ds(base, (NZ - 1) * n), :]
        copy(part, part, zs.at[stage], zr.at[stage], partner).wait_recv()

    def z_drain(stage, ref, n):
        part = ref.at[pl.ds(0, (NZ - 1) * n), :]
        copy(part, part, zs.at[stage], zr.at[stage], partner).wait_send()

    def p_recv(stage, ref, n, base=0):
        part = ref.at[pl.ds(base, (PLANE - 1) * n), :]
        copy(part, part, ps.at[stage], pr.at[stage], partner).wait_recv()

    def p_drain(stage, ref, n):
        part = ref.at[pl.ds(0, (PLANE - 1) * n), :]
        copy(part, part, ps.at[stage], pr.at[stage], partner).wait_send()

    def w_copy(i):
        part = pl.ds(i * (H // W_PARTS), H // W_PARTS)
        return pltpu.make_async_copy(w_hbm.at[part, :], w.at[part, :], w_sem.at[i])

    for i in range(W_PARTS):
        w_copy(i).start()
    mine = rows(c, BANK)
    other = rows(1 - c, BANK)
    own_bank = pltpu.make_async_copy(bank_hbm, bank.at[mine, :], bank_sem)

    barrier = pltpu.get_barrier_semaphore()

    def greet(target):
        pl.semaphore_signal(barrier, inc=1, device_id=(target,), device_id_type=MESH)

    greet(partner)
    z_each(lambda t: greet(z_dev(t)))
    p_each(lambda t: greet(p_dev(t)))
    lane = lax.broadcasted_iota(jnp.int32, (8, LANES), 1)
    sub = lax.broadcasted_iota(jnp.int32, (8, LANES), 0)
    own_lane = lax.rem(p, 8) * BLOCK + z
    tile = jnp.zeros((8, LANES), jnp.int32)
    for r in range(OWN):
        at_row, at_lane = (r // PART) * 2 + p // 8, own_lane + (r % PART) * NZ
        tile = jnp.where((lane == at_lane) & (sub == at_row), pos_ref[r], tile)
    posz[rows(z, 8), :] = tile
    states_f = states_ref[...].astype(F32)
    for zz in range(NZ):
        for yy in range(NY):
            at = (yy * NZ + zz) * LANES
            stz_out[pl.ds(zz * 16 + yy, OWN, stride=NY), :] = states_f[:, at:at + LANES]
    stz_in[rows(z, 16), :] = stz_out[rows(z, 16), :]
    pl.semaphore_wait(barrier, 1 + (NZ - 1) + (PLANE - 1))

    bank_out = copy(bank_hbm, bank.at[mine, :], cs.at[0], cr.at[0], partner)
    z_send(POS, lambda t: slots(posz, 8)(z), slots(posz, 8))
    z_send(STATES, slots(stz_out, 16), slots(stz_in, 16))

    bank_out.start()
    own_bank.start()

    proj = jnp.zeros((OWN, E), F32)
    for i in range(W_PARTS):
        w_copy(i).wait()
        part = slice(i * (H // W_PARTS), (i + 1) * (H // W_PARTS))
        proj = proj + jnp.dot(states_ref[:, part], w[part, :], preferred_element_type=F32)
    radius = jnp.sqrt(jnp.sum(proj * proj, axis=1, keepdims=True) + 1e-06)
    unit = proj / radius
    for e in range(SPLIT):
        unit_s[pl.ds(e, OWN, stride=SPLIT), :] = unit[:, e * LANES:(e + 1) * LANES]
    zq[rows(z, OWN * SPLIT), :] = unit_s[...].astype(BF16)
    zq_at = slots(zq, OWN * SPLIT)
    z_send(QUERY[0], lambda t: zq_at(z), zq_at)
    radius_b = jnp.broadcast_to(radius, (OWN, LANES))
    for e in range(SPLIT):
        uz_out[e * 8:e * 8 + OWN, :] = unit[:, e * LANES:(e + 1) * LANES]
        uz_out[e * 8 + OWN:(e + 1) * 8, :] = radius_b
    uz_in[rows(z, 8), :] = uz_out[rows(z, 8), :]
    z_send(UNIT, slots(uz_out, 8), slots(uz_in, 8))

    z_recv(POS, posz, 8)
    tile = jnp.zeros((8, LANES), jnp.int32)
    for s in range(NZ):
        tile = tile + posz[s * 8:(s + 1) * 8, :]
    posp[rows(p, 8), :] = tile
    p_send(POS, lambda t: slots(posp, 8)(p), slots(posp, 8))
    z_recv(STATES, stz_in, 16)
    for yy in range(NY):
        column_slab = [stz_in[pl.ds(r * NY + yy, NZ, stride=16), :] for r in range(OWN)]
        stp_out[yy * 32:(yy + 1) * 32, :] = jnp.concatenate(column_slab, axis=0).astype(BF16)
    slab[rows(p, 32), :] = stp_out[rows(y, 32), :]

    z_recv(QUERY[0], zq, OWN * SPLIT)

    def gathered(base, step, e):
        block = [zf[pl.ds(base + r * SPLIT + e, NZ, stride=step), :] for r in range(PART)]
        return jnp.concatenate(block, axis=0).astype(BF16)

    x_peers = [lax.rem(x + k, NX) for k in (2, 1, 3)]
    y_peers = [lax.rem(y + k, NY) for k in (2, 1, 3)]

    def p_start(stage, ref, target):
        copy(ref, ref, ps.at[stage], pr.at[stage], target).start()

    zf[...] = zq[...].astype(F32)
    for s in range(SETS):
        for e in range(SPLIT // 2):
            here = slice(e * LANES, (e + 1) * LANES)
            qleft[s * NY + y, x, :, here] = gathered(s * PART * SPLIT, OWN * SPLIT, e)
            qright[s * NY + y, x, :, here] = gathered(s * PART * SPLIT, OWN * SPLIT, SPLIT // 2 + e)
        for i in range(3):
            p_start(LEFT_X[s], qleft.at[s * NY + y, x], dev(y, z, x_peers[i]))
            p_start(RIGHT_Y[s], qright.at[s * NY + y, x], dev(y_peers[i], z, x))

    def q_wait(stage, ref):
        return copy(ref, ref, ps.at[stage], pr.at[stage], partner)

    three_blocks = lambda ref, s: ref.at[s * NY, pl.ds(0, 3)]
    three_lines = lambda ref, s: ref.at[pl.ds(s * NY, 3)]
    for s in range(SETS):
        q_wait(LEFT_X[s], three_blocks(qleft, s)).wait_recv()
        for i in range(3):
            p_start(LEFT_Y[s], qleft.at[s * NY + y], dev(y_peers[i], z, x))
        q_wait(RIGHT_Y[s], three_blocks(qright, s)).wait_recv()
        for i in range(3):
            p_start(RIGHT_X[s], qright.at[pl.ds(s * NY, NY), x], dev(y, z, x_peers[i]))
    p_send(STATES, lambda t: slots(stp_out, 32)(t // NX), slots(slab, 32))
    own_bank.wait()
    copy(bank.at[other, :], bank.at[other, :], cs.at[0], cr.at[0], partner).wait_recv()
    p_recv(POS, posp, 8)
    tile = jnp.zeros((8, LANES), jnp.int32)
    for s in range(PLANE):
        tile = tile + posp[s * 8:(s + 1) * 8, :]
    final[0:8, :] = (tile - chip * (2 * BANK)).astype(F32)

    eye = lax.broadcasted_iota(jnp.int32, (LANES, LANES), 0) == lax.broadcasted_iota(jnp.int32, (LANES, LANES), 1)
    to_row = lambda col: jnp.sum(jnp.where(eye, jnp.broadcast_to(col, (LANES, LANES)), 0.0), axis=0, keepdims=True)
    to_col = lambda row: jnp.sum(jnp.where(eye, jnp.broadcast_to(row, (LANES, LANES)), 0.0), axis=1, keepdims=True)
    tiles = 2 * BANK // TILE
    column = lax.broadcasted_iota(jnp.int32, (SET, LANES), 1)
    two_cols = lambda base: jnp.concatenate([to_col(final[base + h:base + h + 1, :]) for h in range(2)], axis=0)
    hits_of = lambda s: two_cols(s * 2).astype(jnp.int32)

    def pick(s):
        hit_col = hits_of(s)
        for j in range(2 * BANK // LANES):
            coef[:, j * LANES:(j + 1) * LANES] = (column == hit_col - j * LANES).astype(F32).astype(BF16)
        for j in range(E // TILE):
            here = slice(j * TILE, (j + 1) * TILE)
            chosen[s * SET:(s + 1) * SET, here] = jnp.dot(
                coef[...], bank[:, here], preferred_element_type=F32).astype(BF16)

    pick(0)
    pick(1)

    def scores_of(s):
        mine = pl.multiple_of((s * PLANE + p) * 8, 8)
        sp[pl.ds(mine, 8), :] = jnp.zeros((8, LANES), F32)
        q_wait(LEFT_Y[s], three_lines(qleft, s)).wait_recv()
        q_wait(RIGHT_X[s], three_lines(qright, s)).wait_recv()
        at = slice(s * SET, (s + 1) * SET)
        left = qleft[s * NY:(s + 1) * NY].reshape(SET, HALF)
        right = qright[s * NY:(s + 1) * NY].reshape(SET, HALF)
        hit_col = hits_of(s)
        groups = [slice(g * LANES, (g + 1) * LANES) for g in range(TILE // LANES)]
        top, positive = None, jnp.zeros((SET, LANES), F32)
        for j in range(tiles):
            here = slice(j * TILE, (j + 1) * TILE)
            scores = 20.0 * (
                lax.dot_general(left, bank[here, 0:HALF], NT, preferred_element_type=F32)
                + lax.dot_general(right, bank[here, HALF:E], NT, preferred_element_type=F32)
            )
            expo[at, here] = scores
            for g in groups:
                part = scores[:, g]
                top = part if top is None else jnp.maximum(top, part)
                positive = positive + jnp.where(column == hit_col - (j * TILE + g.start), part, 0.0)
        top = jnp.max(top, axis=1, keepdims=True)
        total = jnp.zeros((SET, LANES), F32)
        for j in range(tiles):
            here = slice(j * TILE, (j + 1) * TILE)
            value = jnp.exp(expo[at, here] - top)
            expo[at, here] = value
            for g in groups:
                total = total + value[:, g]
        total = jnp.sum(total, axis=1, keepdims=True)
        for h in range(2):
            half = slice(h * LANES, (h + 1) * LANES)
            sp[pl.ds(mine + h, 1), :] = to_row(top[half, :])
            sp[pl.ds(mine + 2 + h, 1), :] = to_row(total[half, :])
        sp[pl.ds(mine + 4, 1), :] = jnp.sum(positive, axis=0, keepdims=True)
        final[8 + s * 8:16 + s * 8, :] = sp[pl.ds(mine, 8), :]
        at = slots(sp, 8, s * PLANE * 8)
        p_send(STATS[s], lambda t: at(p), at)

    def combine(ref, base, n):
        high = ref[base:base + 8, :]
        found = high
        for i in range(1, n):
            part = ref[base + i * 8:base + i * 8 + 8, :]
            high = jnp.maximum(high, part)
            found = found + part
        total = jnp.zeros((2, LANES), F32)
        for i in range(n):
            total = total + ref[base + i * 8 + 2:base + i * 8 + 4, :] * jnp.exp(
                ref[base + i * 8:base + i * 8 + 2, :] - high[0:2, :]
            )
        return high[0:2, :], total, found[4:5, :]

    def plane_stats(s):
        p_recv(STATS[s], sp, 8, s * PLANE * 8)
        high, total, found = combine(sp, s * PLANE * 8, PLANE)
        at = pl.multiple_of((s * NZ + z) * 8, 8)
        sz[pl.ds(at, 2), :] = high
        sz[pl.ds(at + 2, 2), :] = total
        sz[pl.ds(at + 4, 4), :] = jnp.concatenate([found, jnp.zeros((3, LANES), F32)], axis=0)
        there = slots(sz, 8, s * NZ * 8)
        z_send(STATS[s], lambda t: there(z), there)

    def all_stats(s):
        z_recv(STATS[s], sz, 8, s * NZ * 8)
        high, total, found = combine(sz, s * NZ * 8, NZ)
        lse = high + jnp.log(total)
        here = 8 + s * 8
        final[here + 2:here + 4, :] = jnp.exp(final[here:here + 2, :] - lse)
        final[here + 4:here + 6, :] = high
        return jnp.sum(lse, axis=0, keepdims=True) - found

    def rough_grad(s):
        at = slice(s * SET, (s + 1) * SET)
        hit_col = hits_of(s)
        own = jnp.zeros((SET, LANES), F32)
        for j in range(2 * BANK // LANES):
            here = slice(j * LANES, (j + 1) * LANES)
            hit = column == hit_col - j * LANES
            value = expo[at, here]
            own = own + jnp.where(hit, value, 0.0)
            coef[:, here] = jnp.where(hit, 0.0, value).astype(BF16)
        for j in range(E // TILE):
            here = slice(j * TILE, (j + 1) * TILE)
            pre[at, here] = jnp.dot(coef[...], bank[:, here], preferred_element_type=F32)
        return jnp.sum(own, axis=1, keepdims=True)

    def grad_of(s, own):
        at = slice(s * SET, (s + 1) * SET)
        scale_col = two_cols(8 + s * 8 + 2)
        positive_col = 20.0 * ((own * scale_col - 1.0) * (1.0 / QUERIES)).astype(BF16).astype(F32)
        scale_col = scale_col * (20.0 / QUERIES)
        for j in range(SPLIT):
            here = slice(j * LANES, (j + 1) * LANES)
            gout[at, here] = (pre[at, here] * scale_col + chosen[at, here].astype(F32) * positive_col).astype(BF16)
        p_send(GRAD[s], slots(gout, BLOCK, s * SET), slots(gin, BLOCK, s * SET))
        gin[rows(p, BLOCK, s * SET), :] = gout[rows(p, BLOCK, s * SET), :]

    scores_of(0)
    scores_of(1)
    own_0 = rough_grad(0)
    plane_stats(0)
    own_1 = rough_grad(1)
    plane_stats(1)
    lost = all_stats(0)
    grad_of(0, own_0)
    lost = lost + all_stats(1)
    grad_of(1, own_1)
    lossbuf[0:8, :] = jnp.broadcast_to(jnp.sum(lost), (8, LANES))
    loss_out = copy(lossbuf.at[0:8, :], lossbuf.at[8:16, :], cs.at[1], cr.at[1], partner)
    loss_out.start()

    top_tile = jnp.zeros((8, LANES), F32)
    for r in range(OWN):
        row = final[pl.ds(8 + (r // PART) * 8 + 4 + p // 8, 1), :]
        mask = lax.broadcasted_iota(jnp.int32, (1, LANES), 1) == own_lane + (r % PART) * NZ
        value = jnp.sum(jnp.where(mask, row, 0.0))
        top_tile = jnp.where(lane == r, value, top_tile)
    top_ref[...] = top_tile
    p_recv(STATES, slab, 32)
    for s in range(SETS):
        part = slab[...].astype(F32).reshape(PLANE, 32, LANES)[:, s * BLOCK:(s + 1) * BLOCK, :].reshape(SET, LANES)
        turn[...] = jnp.transpose(part)
        turned[rows(z, 32), s * SET:(s + 1) * SET] = turn[rows(x, 32), :].astype(BF16)
    z_send(TURNED, lambda t: slots(turned, 32)(z), slots(turned, 32))

    def line_grad(s):
        p_recv(GRAD[s], gin, BLOCK, s * SET)

        def add(i, acc):
            return acc + gin[rows(i, BLOCK, s * SET), :].astype(F32)

        acc = lax.fori_loop(0, PLANE, add, jnp.zeros((BLOCK, E), F32))
        query = jnp.concatenate([qleft[s * NY + y, x], qright[s * NY + y, x]], axis=1).astype(F32)
        inner = jnp.sum(query * acc, axis=1, keepdims=True)
        inner = jnp.where(lane == 0, inner[0:NZ, :], jnp.where(lane == 1, inner[NZ:2 * NZ, :], 0.0))
        base = s * NZ * 24
        for e in range(SPLIT):
            gz_out[base + e * 24:base + e * 24 + BLOCK, :] = acc[:, e * LANES:(e + 1) * LANES]
            gz_out[base + e * 24 + BLOCK:base + (e + 1) * 24, :] = inner
        z_send(GRAD[s], slots(gz_out, 24, base), slots(gz_in, 24, base))
        gz_in[rows(z, 24, base), :] = gz_out[rows(z, 24, base), :]

    def slice_grad(s):
        base = s * NZ * 24
        z_recv(GRAD[s], gz_in, 24, base)
        grad = gz_in[base:base + 24, :]
        for i in range(1, NZ):
            grad = grad + gz_in[base + i * 24:base + (i + 1) * 24, :]
        block = []
        for r in range(PART):
            inner = jnp.sum(jnp.where(lane == r, grad[BLOCK:24, :], 0.0), axis=1, keepdims=True)
            u = uz_in[pl.ds(s * PART + r, NZ, stride=8), :]
            radius = uz_in[pl.ds(OWN + s * PART + r, NZ, stride=8), :]
            block.append((grad[r * NZ:(r + 1) * NZ, :] - u * inner) / radius)
        rounded = jnp.concatenate(block, axis=0).astype(BF16)
        gpall[rows(p, BLOCK, s * SET), :] = rounded
        at = slots(gpall, BLOCK, s * SET)
        p_send(PROJ[s], lambda t: at(p), at)
        for r in range(PART):
            gs_out[pl.ds(s * PART + r, NZ, stride=8), :] = rounded.astype(F32)[r * NZ:(r + 1) * NZ, :]

    gs_out[...] = jnp.zeros_like(gs_out)
    line_grad(0)
    line_grad(1)
    z_recv(UNIT, uz_in, 8)
    slice_grad(0)
    slice_grad(1)
    z_send(OWNERS, slots(gs_out, 8), slots(gs_in, 8))
    gs_in[rows(z, 8), :] = gs_out[rows(z, 8), :]

    z_drain(POS, posz, 8)
    z_drain(STATES, stz_out, 16)
    z_drain(QUERY[0], zq, OWN * SPLIT)
    z_drain(UNIT, uz_out, 8)
    p_drain(POS, posp, 8)
    p_drain(STATES, slab, 32)
    for s in range(SETS):
        z_drain(STATS[s], sz, 8)
        z_drain(GRAD[s], gz_out, 24)
        q_wait(LEFT_X[s], three_blocks(qleft, s)).wait_send()
        q_wait(LEFT_Y[s], three_lines(qleft, s)).wait_send()
        q_wait(RIGHT_Y[s], three_blocks(qright, s)).wait_send()
        q_wait(RIGHT_X[s], three_lines(qright, s)).wait_send()
        p_drain(STATS[s], sp, 8)
        p_drain(GRAD[s], gout, BLOCK)
    bank_out.wait_send()
    loss_out.wait()
    loss_ref[...] = (lossbuf[0:8, :] + lossbuf[8:16, :]) * (1.0 / QUERIES)

    z_recv(TURNED, turned, 32)
    p_recv(PROJ[0], gpall, BLOCK, 0)
    weight = jnp.dot(turned[:, 0:SET], gpall[0:SET, :], preferred_element_type=F32)
    p_recv(PROJ[1], gpall, BLOCK, SET)
    weight = weight + jnp.dot(turned[:, SET:ROWS], gpall[SET:ROWS, :], preferred_element_type=F32)
    gw_all[...] = weight.reshape(NZ, 32, LANES)
    core_out = copy(gw_all.at[:, rows(1 - c, 16), :], gw_in, cs.at[2], cr.at[2], partner)
    core_out.start()
    z_drain(TURNED, turned, 32)
    p_drain(PROJ[0], gpall, BLOCK)
    p_drain(PROJ[1], gpall, BLOCK)
    core_out.wait()
    gw_out[...] = (gw_all[:, rows(c, 16), :] + gw_in[...]).reshape(NZ * 16, LANES)
    z_send(WEIGHT, slots(gw_out, 16), slots(gw_parts, 16))
    gw_parts[rows(z, 16), :] = gw_out[rows(z, 16), :]

    z_recv(OWNERS, gs_in, 8)
    gp = jnp.concatenate([gs_in[e * 8:e * 8 + OWN, :] for e in range(SPLIT)], axis=1).astype(BF16)
    for j in range(H // TILE):
        here = slice(j * TILE, (j + 1) * TILE)
        gs_ref[:, here] = lax.dot_general(gp, w[here, :], NT, preferred_element_type=F32).astype(BF16)
    z_drain(OWNERS, gs_out, 8)
    z_recv(WEIGHT, gw_parts, 16)
    for e in range(SPLIT):
        gw_ref[:, e * LANES:(e + 1) * LANES] = gw_parts[e * 16:(e + 1) * 16, :]
    z_drain(WEIGHT, gw_out, 16)


def hand_over(loss_in, top_in, gs_in, gw_in, loss_ref, top_ref, gs_ref, gw_ref):
    loss_ref[...] = loss_in[0:1, 0:1]
    top_ref[...] = top_in[0:1, 0:OWN]
    gs_ref[...] = gs_in[...]
    gw_ref[...] = gw_in[...]


def local(states, head_weight, bank, positive_index):
    vmem = pltpu.VMEM
    dma = pltpu.SemaphoreType.DMA
    in_vmem = pl.BlockSpec(memory_space=pltpu.VMEM)
    grads = (jax.ShapeDtypeStruct((OWN, H), BF16), jax.ShapeDtypeStruct((16, E), F32))
    parts = pl.pallas_call(
        kernel,
        out_shape=(jax.ShapeDtypeStruct((8, LANES), F32),) * 2 + grads,
        in_specs=[
            in_vmem,
            pl.BlockSpec(memory_space=pl.ANY),
            pl.BlockSpec(memory_space=pl.ANY),
            pl.BlockSpec(memory_space=pltpu.SMEM),
        ],
        out_specs=(in_vmem,) * 4,
        scratch_shapes=[
            vmem((H, E), BF16),
            vmem((2 * BANK, E), BF16),
            vmem((NZ * 8, LANES), jnp.int32),
            vmem((PLANE * 8, LANES), jnp.int32),
            vmem((NZ * 16, LANES), F32),
            vmem((NZ * 16, LANES), F32),
            vmem((NY * 32, LANES), BF16),
            vmem((ROWS, LANES), BF16),
            vmem((NZ * 32, ROWS), BF16),
            vmem((LANES, SET), F32),
            vmem((NZ * OWN * SPLIT, LANES), BF16),
            vmem((NZ * OWN * SPLIT, LANES), F32),
            vmem((OWN * SPLIT, LANES), F32),
            vmem((NZ * 8, LANES), F32),
            vmem((NZ * 8, LANES), F32),
            vmem((SETS * NY, NX, BLOCK, HALF), BF16),
            vmem((SETS * NY, NX, BLOCK, HALF), BF16),
            vmem((ROWS, 2 * BANK), F32),
            vmem((SET, 2 * BANK), BF16),
            vmem((ROWS, E), F32),
            vmem((ROWS, E), BF16),
            vmem((SETS * PLANE * 8, LANES), F32),
            vmem((SETS * NZ * 8, LANES), F32),
            vmem((24, LANES), F32),
            vmem((ROWS, E), BF16),
            vmem((ROWS, E), BF16),
            vmem((SETS * NZ * 24, LANES), F32),
            vmem((SETS * NZ * 24, LANES), F32),
            vmem((NZ * 8, LANES), F32),
            vmem((NZ * 8, LANES), F32),
            vmem((ROWS, LANES), BF16),
            vmem((NZ, 32, LANES), F32),
            vmem((NZ, 16, LANES), F32),
            vmem((NZ * 16, LANES), F32),
            vmem((NZ * 16, LANES), F32),
            vmem((16, LANES), F32),
            dma((W_PARTS,)), dma,
            dma((3,)), dma((3,)),
            dma((STAGES,)), dma((STAGES,)),
            dma((STAGES,)), dma((STAGES,)),
        ],
        compiler_params=pltpu.CompilerParams(
            collective_id=0, has_side_effects=True, vmem_limit_bytes=56 * 2**20
        ),
        name="info_nce",
    )(states, head_weight, bank, positive_index)
    loss, top, grad_states, grad_weight = pl.pallas_call(
        hand_over,
        out_shape=(jax.ShapeDtypeStruct((1, 1), F32), jax.ShapeDtypeStruct((1, OWN), F32)) + grads,
        in_specs=[in_vmem] * 4,
        out_specs=(in_vmem,) * 4,
        name="hand_over",
    )(*parts)
    return (loss.reshape(()), top.reshape((OWN,)), grad_states, grad_weight)


def solution(mesh):
    placed = (P("dev", None), P(), P("dev", None), P("dev"))
    return jax.shard_map(
        local,
        mesh=mesh,
        in_specs=placed,
        out_specs=(P(), P("dev"), P("dev", None), P("dev", None)),
        check_vma=False,
    )
```

```python
import jax
import jax.numpy as jnp
from jax import lax
from jax.experimental import pallas as pl
from jax.experimental.pallas import tpu as pltpu
from jax.sharding import PartitionSpec as P

NY, NZ, NX = 4, 8, 4
PLANE = NY * NX
OWN = 4
SETS = 2
PART = OWN // SETS
H, E = 4096, 1024
BANK = 1024
BLOCK = NZ * PART
SET = PLANE * BLOCK
ROWS = SETS * SET
LANES = 128
SPLIT = E // LANES
TILE = 512
W_PARTS = 8
QUERIES = 1024
MESH = pl.DeviceIdType.MESH
NT = (((1,), (1,)), ((), ()))
POS, STATES = 0, 1
QUERY, STATS, GRAD, PROJ = (2, 3), (4, 5), (6, 7), (8, 9)
DIRECT, LEFT, RIGHT = (2, 3), (10, 11), (12, 13)
UNIT, TURNED, OWNERS, WEIGHT, ACROSS = 3, 10, 8, 9, 11
STAGES = 16
HALF = E // 2
F32, BF16 = jnp.float32, jnp.bfloat16


def kernel(
    states_ref, w_hbm, bank_hbm, pos_ref,
    loss_ref, top_ref, gs_ref, gw_ref,
    w, bank, posz, posp, stz_out, stz_in, stp_out, slab, turned, turn,
    zq, zf, unit_s, uz_out, uz_in, qall, expo, coef, pre, chosen, sp, sz, final, gout, gin,
    gz_out, gz_in, gs_out, gs_in, gpall, gw_all, gw_parts, lossbuf,
    w_sem, bank_sem, cs, cr, zs, zr, ps, pr, qr,
):
    me = lax.axis_index("dev")
    c = lax.rem(me, 2)
    x = lax.rem(me // 2, NX)
    z = lax.rem(me // (2 * NX), NZ)
    y = me // (2 * NX * NZ)
    p = y * NX + x
    chip = me // 2
    partner = chip * 2 + (1 - c)

    def dev(yy, zz, xx):
        return ((yy * NZ + zz) * NX + xx) * 2 + c

    def rows(i, n, base=0):
        return pl.ds(pl.multiple_of(base + i * n, n), n)

    def slots(ref, n, base=0):
        return lambda s: ref.at[rows(s, n, base), :]

    def copy(src, dst, send_sem, recv_sem, target):
        return pltpu.make_async_remote_copy(
            src_ref=src, dst_ref=dst, send_sem=send_sem, recv_sem=recv_sem,
            device_id=(target,), device_id_type=MESH,
        )

    def away(k):
        return 2 * (1 - k % 2) + (k % 2 + k // 2) % 2

    def each(n, body, short):
        if short:
            lax.fori_loop(0, n, lambda k, carry: (body(k), carry)[1], 0)
        else:
            for k in range(n):
                body(k)

    def z_each(body, short=False):
        each(NZ - 1, lambda k: body(lax.rem(z + 4 + (k // 2 + k % 2) * (1 - 2 * (k % 2)), NZ)), short)

    def p_each(body, short=False):
        each(PLANE - 1, lambda k: body(
            lax.rem(y + away(k // NX), NY) * NX + lax.rem(x + away(k % NX), NX)), short)

    z_dev = lambda t: dev(y, t, x)
    p_dev = lambda t: dev(t // NX, z, lax.rem(t, NX))
    across = lambda t: dev(y, t, x) + 1 - 2 * c

    def z_send(stage, src, dst, short=False):
        z_each(lambda t: copy(src(t), dst(z), zs.at[stage], zr.at[stage], z_dev(t)).start(), short)

    def p_send(stage, src, dst, short=False):
        p_each(lambda t: copy(src(t), dst(p), ps.at[stage], pr.at[stage], p_dev(t)).start(), short)

    def z_recv(stage, ref, n, base=0):
        part = ref.at[pl.ds(base, (NZ - 1) * n), :]
        copy(part, part, zs.at[stage], zr.at[stage], partner).wait_recv()

    def z_drain(stage, ref, n):
        part = ref.at[pl.ds(0, (NZ - 1) * n), :]
        copy(part, part, zs.at[stage], zr.at[stage], partner).wait_send()

    def p_recv(stage, ref, n, base=0):
        part = ref.at[pl.ds(base, (PLANE - 1) * n), :]
        copy(part, part, ps.at[stage], pr.at[stage], partner).wait_recv()

    def p_drain(stage, ref, n):
        part = ref.at[pl.ds(0, (PLANE - 1) * n), :]
        copy(part, part, ps.at[stage], pr.at[stage], partner).wait_send()

    def w_copy(i):
        part = pl.ds(i * (H // W_PARTS), H // W_PARTS)
        return pltpu.make_async_copy(w_hbm.at[part, :], w.at[part, :], w_sem.at[i])

    for i in range(W_PARTS):
        w_copy(i).start()
    mine = rows(c, BANK)
    other = rows(1 - c, BANK)
    own_bank = pltpu.make_async_copy(bank_hbm, bank.at[mine, :], bank_sem)

    barrier = pltpu.get_barrier_semaphore()

    def greet(target):
        pl.semaphore_signal(barrier, inc=1, device_id=(target,), device_id_type=MESH)

    greet(partner)
    z_each(lambda t: greet(z_dev(t)), True)
    z_each(lambda t: greet(across(t)), True)
    p_each(lambda t: greet(p_dev(t)), True)
    lane = lax.broadcasted_iota(jnp.int32, (8, LANES), 1)
    sub = lax.broadcasted_iota(jnp.int32, (8, LANES), 0)
    own_lane = lax.rem(p, 8) * BLOCK + z
    tile = jnp.zeros((8, LANES), jnp.int32)
    for r in range(OWN):
        at_row, at_lane = (r // PART) * 2 + p // 8, own_lane + (r % PART) * NZ
        tile = jnp.where((lane == at_lane) & (sub == at_row), pos_ref[r], tile)
    posz[rows(z, 8), :] = tile
    states_f = states_ref[...].astype(F32)
    for zz in range(NZ):
        for yy in range(NY):
            at = (yy * NZ + zz) * LANES
            stz_out[pl.ds(zz * 16 + yy, OWN, stride=NY), :] = states_f[:, at:at + LANES]
    stz_in[rows(z, 16), :] = stz_out[rows(z, 16), :]
    pl.semaphore_wait(barrier, 1 + 2 * (NZ - 1) + (PLANE - 1))

    bank_out = copy(bank_hbm, bank.at[mine, :], cs.at[0], cr.at[0], partner)
    z_send(POS, lambda t: slots(posz, 8)(z), slots(posz, 8), True)
    z_send(STATES, slots(stz_out, 16), slots(stz_in, 16), True)

    bank_out.start()
    own_bank.start()

    proj = jnp.zeros((OWN, E), F32)
    for i in range(W_PARTS):
        w_copy(i).wait()
        part = slice(i * (H // W_PARTS), (i + 1) * (H // W_PARTS))
        proj = proj + jnp.dot(states_ref[:, part], w[part, :], preferred_element_type=F32)
    radius = jnp.sqrt(jnp.sum(proj * proj, axis=1, keepdims=True) + 1e-06)
    unit = proj / radius
    for e in range(SPLIT):
        unit_s[pl.ds(e, OWN, stride=SPLIT), :] = unit[:, e * LANES:(e + 1) * LANES]
    zq[rows(z, OWN * SPLIT), :] = unit_s[...].astype(BF16)
    zq_at = slots(zq, OWN * SPLIT)
    z_send(QUERY[0], lambda t: zq_at(z), zq_at)
    radius_b = jnp.broadcast_to(radius, (OWN, LANES))
    for e in range(SPLIT):
        uz_out[e * 8:e * 8 + OWN, :] = unit[:, e * LANES:(e + 1) * LANES]
        uz_out[e * 8 + OWN:(e + 1) * 8, :] = radius_b
    uz_in[rows(z, 8), :] = uz_out[rows(z, 8), :]
    z_send(UNIT, slots(uz_out, 8), slots(uz_in, 8), True)

    z_recv(POS, posz, 8)
    tile = jnp.zeros((8, LANES), jnp.int32)
    for s in range(NZ):
        tile = tile + posz[s * 8:(s + 1) * 8, :]
    posp[rows(p, 8), :] = tile
    p_send(POS, lambda t: slots(posp, 8)(p), slots(posp, 8), True)
    z_recv(STATES, stz_in, 16)
    for yy in range(NY):
        column_slab = [stz_in[pl.ds(r * NY + yy, NZ, stride=16), :] for r in range(OWN)]
        stp_out[yy * 32:(yy + 1) * 32, :] = jnp.concatenate(column_slab, axis=0).astype(BF16)
    slab[rows(p, 32), :] = stp_out[rows(y, 32), :]

    z_recv(QUERY[0], zq, OWN * SPLIT)

    def gathered(base, step, e):
        block = [zf[pl.ds(base + r * SPLIT + e, NZ, stride=step), :] for r in range(PART)]
        return jnp.concatenate(block, axis=0).astype(BF16)

    def q_copy(stage, ref, target, recv_sem):
        return copy(ref, ref, ps.at[stage], recv_sem, target)

    zf[...] = zq[...].astype(F32)
    for s in range(SETS):
        for e in range(SPLIT):
            at = e % (SPLIT // 2) * LANES
            qall[s * NY + y, x, e // (SPLIT // 2), :, at:at + LANES] = gathered(s * PART * SPLIT, OWN * SPLIT, e)
        own = qall.at[s * NY + y, x]
        for k in (2, 1, 3):
            q_copy(DIRECT[s], own, dev(y, z, lax.rem(x + k, NX)), qr.at[s, k]).start()
            q_copy(DIRECT[s], own, dev(lax.rem(y + k, NY), z, x), qr.at[s, NX + k]).start()
    own_bank.wait()
    copy(bank.at[other, :], bank.at[other, :], cs.at[0], cr.at[0], partner).wait_recv()
    p_recv(POS, posp, 8)
    tile = jnp.zeros((8, LANES), jnp.int32)
    for s in range(PLANE):
        tile = tile + posp[s * 8:(s + 1) * 8, :]
    final[0:8, :] = (tile - chip * (2 * BANK)).astype(F32)

    eye = lax.broadcasted_iota(jnp.int32, (LANES, LANES), 0) == lax.broadcasted_iota(jnp.int32, (LANES, LANES), 1)
    to_row = lambda col: jnp.sum(jnp.where(eye, jnp.broadcast_to(col, (LANES, LANES)), 0.0), axis=0, keepdims=True)
    to_col = lambda row: jnp.sum(jnp.where(eye, jnp.broadcast_to(row, (LANES, LANES)), 0.0), axis=1, keepdims=True)
    tiles = 2 * BANK // TILE
    column = lax.broadcasted_iota(jnp.int32, (SET, LANES), 1)
    two_cols = lambda base: jnp.concatenate([to_col(final[base + h:base + h + 1, :]) for h in range(2)], axis=0)
    hits_of = lambda s: two_cols(s * 2).astype(jnp.int32)

    def pick(s):
        at = slice(s * SET, (s + 1) * SET)
        hit_at = hits_of(s) - column
        for j in range(2 * BANK // LANES):
            coef[at, j * LANES:(j + 1) * LANES] = (hit_at == j * LANES).astype(F32).astype(BF16)
        for j in range(E // TILE):
            here = slice(j * TILE, (j + 1) * TILE)
            chosen[at, here] = jnp.dot(coef[at, :], bank[:, here], preferred_element_type=F32).astype(BF16)

    pick(0)

    for s in range(SETS):
        for k in (1, 3, 2):
            came = qall.at[s * NY + y, lax.rem(x + NX - k, NX)]
            q_copy(DIRECT[s], came, partner, qr.at[s, k]).wait_recv()
            for m in (2, 1, 3):
                q_copy(LEFT[s], came.at[0], dev(lax.rem(y + m, NY), z, x), pr.at[LEFT[s]]).start()
            came = qall.at[s * NY + lax.rem(y + NY - k, NY), x]
            q_copy(DIRECT[s], came, partner, qr.at[s, NX + k]).wait_recv()
            for m in (2, 1, 3):
                q_copy(RIGHT[s], came.at[1], dev(y, z, lax.rem(x + m, NX)), pr.at[RIGHT[s]]).start()

    p_send(STATES, lambda t: slots(stp_out, 32)(t // NX), slots(slab, 32), True)
    pick(1)

    def q_wait(stage, s):
        nine = qall.at[pl.ds(s * NY, 3), pl.ds(0, 3), 0]
        return copy(nine, nine, ps.at[stage], pr.at[stage], partner)

    def scores_of(s):
        mine = pl.multiple_of((s * PLANE + p) * 8, 8)
        sp[pl.ds(mine, 8), :] = jnp.zeros((8, LANES), F32)
        q_wait(LEFT[s], s).wait_recv()
        q_wait(RIGHT[s], s).wait_recv()
        at = slice(s * SET, (s + 1) * SET)
        left = qall[s * NY:(s + 1) * NY, :, 0].reshape(SET, HALF)
        right = qall[s * NY:(s + 1) * NY, :, 1].reshape(SET, HALF)
        hit_at = hits_of(s) - column
        top = None
        for j in range(tiles):
            here = slice(j * TILE, (j + 1) * TILE)
            scores = 20.0 * (
                lax.dot_general(left, bank[here, 0:HALF], NT, preferred_element_type=F32)
                + lax.dot_general(right, bank[here, HALF:E], NT, preferred_element_type=F32)
            )
            expo[:, here] = scores
            for g in range(TILE // LANES):
                part = scores[:, g * LANES:(g + 1) * LANES]
                top = part if top is None else jnp.maximum(top, part)
        top = jnp.max(top, axis=1, keepdims=True)
        total = positive = jnp.zeros((SET, LANES), F32)
        for j in range(2 * BANK // LANES):
            here = slice(j * LANES, (j + 1) * LANES)
            score = expo[:, here]
            value = jnp.exp(score - top)
            hit = hit_at == j * LANES
            total = total + value
            positive = positive + jnp.where(hit, score, 0.0)
            coef[at, here] = jnp.where(hit, 0.0, value).astype(BF16)
        total = jnp.sum(total, axis=1, keepdims=True)
        for h in range(2):
            half = slice(h * LANES, (h + 1) * LANES)
            sp[pl.ds(mine + h, 1), :] = to_row(top[half, :])
            sp[pl.ds(mine + 2 + h, 1), :] = to_row(total[half, :])
        sp[pl.ds(mine + 4, 1), :] = jnp.sum(positive, axis=0, keepdims=True)
        final[8 + s * 8:16 + s * 8, :] = sp[pl.ds(mine, 8), :]
        at = slots(sp, 8, s * PLANE * 8)
        p_send(STATS[s], lambda t: at(p), at)
        return jnp.exp(jnp.minimum(jnp.sum(positive, axis=1, keepdims=True) - top, 0.0))

    def combine(ref, base, n):
        high = ref[base:base + 8, :]
        found = high
        for i in range(1, n):
            part = ref[base + i * 8:base + i * 8 + 8, :]
            high = jnp.maximum(high, part)
            found = found + part
        total = jnp.zeros((2, LANES), F32)
        for i in range(n):
            total = total + ref[base + i * 8 + 2:base + i * 8 + 4, :] * jnp.exp(
                ref[base + i * 8:base + i * 8 + 2, :] - high[0:2, :]
            )
        return high[0:2, :], total, found[4:5, :]

    def plane_stats(s):
        p_recv(STATS[s], sp, 8, s * PLANE * 8)
        high, total, found = combine(sp, s * PLANE * 8, PLANE)
        at = pl.multiple_of((s * NZ + z) * 8, 8)
        sz[pl.ds(at, 2), :] = high
        sz[pl.ds(at + 2, 2), :] = total
        sz[pl.ds(at + 4, 4), :] = jnp.concatenate([found, jnp.zeros((3, LANES), F32)], axis=0)
        there = slots(sz, 8, s * NZ * 8)
        z_send(STATS[s], lambda t: there(z), there)

    def all_stats(s):
        z_recv(STATS[s], sz, 8, s * NZ * 8)
        high, total, found = combine(sz, s * NZ * 8, NZ)
        lse = high + jnp.log(total)
        here = 8 + s * 8
        final[here + 2:here + 4, :] = jnp.exp(final[here:here + 2, :] - lse)
        final[here + 4:here + 6, :] = high
        return jnp.sum(lse, axis=0, keepdims=True) - found

    def rough_grad(s):
        at = slice(s * SET, (s + 1) * SET)
        for j in range(E // TILE):
            here = slice(j * TILE, (j + 1) * TILE)
            pre[at, here] = jnp.dot(coef[at, :], bank[:, here], preferred_element_type=F32)

    def grad_of(s, own):
        at = slice(s * SET, (s + 1) * SET)
        scale_col = two_cols(8 + s * 8 + 2)
        positive_col = 20.0 * ((own * scale_col - 1.0) * (1.0 / QUERIES)).astype(BF16).astype(F32)
        scale_col = scale_col * (20.0 / QUERIES)
        for j in range(SPLIT):
            here = slice(j * LANES, (j + 1) * LANES)
            gout[at, here] = (pre[at, here] * scale_col + chosen[at, here].astype(F32) * positive_col).astype(BF16)
        p_send(GRAD[s], slots(gout, BLOCK, s * SET), slots(gin, BLOCK, s * SET))
        gin[rows(p, BLOCK, s * SET), :] = gout[rows(p, BLOCK, s * SET), :]

    own_0 = scores_of(0)
    own_1 = scores_of(1)
    rough_grad(0)
    plane_stats(0)
    rough_grad(1)
    plane_stats(1)
    lost = all_stats(0)
    grad_of(0, own_0)
    lost = lost + all_stats(1)
    grad_of(1, own_1)
    lossbuf[0:8, :] = jnp.broadcast_to(jnp.sum(lost), (8, LANES))
    loss_out = copy(lossbuf.at[0:8, :], lossbuf.at[8:16, :], cs.at[1], cr.at[1], partner)
    loss_out.start()

    top_tile = jnp.zeros((8, LANES), F32)
    for r in range(OWN):
        row = final[pl.ds(8 + (r // PART) * 8 + 4 + p // 8, 1), :]
        mask = lax.broadcasted_iota(jnp.int32, (1, LANES), 1) == own_lane + (r % PART) * NZ
        value = jnp.sum(jnp.where(mask, row, 0.0))
        top_tile = jnp.where(lane == r, value, top_tile)
    top_ref[...] = top_tile
    p_recv(STATES, slab, 32)
    for s in range(SETS):
        part = slab[...].astype(F32).reshape(PLANE, 32, LANES)[:, s * BLOCK:(s + 1) * BLOCK, :].reshape(SET, LANES)
        turn[...] = jnp.transpose(part)
        turned[rows(z, 32), s * SET:(s + 1) * SET] = turn[rows(x, 32), :].astype(BF16)
    z_send(TURNED, lambda t: slots(turned, 32)(z), slots(turned, 32), True)

    def line_grad(s):
        p_recv(GRAD[s], gin, BLOCK, s * SET)

        def add(i, acc):
            return acc + gin[rows(i, BLOCK, s * SET), :].astype(F32)

        acc = lax.fori_loop(0, PLANE, add, jnp.zeros((BLOCK, E), F32))
        query = jnp.concatenate([qall[s * NY + y, x, 0], qall[s * NY + y, x, 1]], axis=1).astype(F32)
        inner = jnp.sum(query * acc, axis=1, keepdims=True)
        inner = jnp.where(lane == 0, inner[0:NZ, :], jnp.where(lane == 1, inner[NZ:2 * NZ, :], 0.0))
        base = s * NZ * 24
        for e in range(SPLIT):
            gz_out[base + e * 24:base + e * 24 + BLOCK, :] = acc[:, e * LANES:(e + 1) * LANES]
            gz_out[base + e * 24 + BLOCK:base + (e + 1) * 24, :] = inner
        z_send(GRAD[s], slots(gz_out, 24, base), slots(gz_in, 24, base))
        gz_in[rows(z, 24, base), :] = gz_out[rows(z, 24, base), :]

    def slice_grad(s):
        base = s * NZ * 24
        z_recv(GRAD[s], gz_in, 24, base)
        grad = gz_in[base:base + 24, :]
        for i in range(1, NZ):
            grad = grad + gz_in[base + i * 24:base + (i + 1) * 24, :]
        block = []
        for r in range(PART):
            inner = jnp.sum(jnp.where(lane == r, grad[BLOCK:24, :], 0.0), axis=1, keepdims=True)
            u = uz_in[pl.ds(s * PART + r, NZ, stride=8), :]
            radius = uz_in[pl.ds(OWN + s * PART + r, NZ, stride=8), :]
            block.append((grad[r * NZ:(r + 1) * NZ, :] - u * inner) / radius)
        rounded = jnp.concatenate(block, axis=0).astype(BF16)
        gpall[rows(p, BLOCK, s * SET), :] = rounded
        at = slots(gpall, BLOCK, s * SET)
        p_send(PROJ[s], lambda t: at(p), at)
        for r in range(PART):
            gs_out[pl.ds(s * PART + r, NZ, stride=8), :] = rounded.astype(F32)[r * NZ:(r + 1) * NZ, :]

    gs_out[...] = jnp.zeros_like(gs_out)
    line_grad(0)
    line_grad(1)
    z_recv(UNIT, uz_in, 8)
    slice_grad(0)
    slice_grad(1)
    z_send(OWNERS, slots(gs_out, 8), slots(gs_in, 8), True)
    gs_in[rows(z, 8), :] = gs_out[rows(z, 8), :]

    z_drain(POS, posz, 8)
    z_drain(STATES, stz_out, 16)
    z_drain(QUERY[0], zq, OWN * SPLIT)
    z_drain(UNIT, uz_out, 8)
    p_drain(POS, posp, 8)
    p_drain(STATES, slab, 32)
    for s in range(SETS):
        z_drain(STATS[s], sz, 8)
        z_drain(GRAD[s], gz_out, 24)
        q_copy(DIRECT[s], qall.at[pl.ds(s * NY, 2), pl.ds(0, 3)], partner, pr.at[DIRECT[s]]).wait_send()
        q_wait(LEFT[s], s).wait_send()
        q_wait(RIGHT[s], s).wait_send()
        p_drain(STATS[s], sp, 8)
        p_drain(GRAD[s], gout, BLOCK)
    bank_out.wait_send()
    loss_out.wait()
    loss_ref[...] = (lossbuf[0:8, :] + lossbuf[8:16, :]) * (1.0 / QUERIES)

    z_recv(TURNED, turned, 32)
    p_recv(PROJ[0], gpall, BLOCK, 0)
    weight = jnp.dot(turned[:, 0:SET], gpall[0:SET, :], preferred_element_type=F32)
    p_recv(PROJ[1], gpall, BLOCK, SET)
    weight = weight + jnp.dot(turned[:, SET:ROWS], gpall[SET:ROWS, :], preferred_element_type=F32)
    gw_all[...] = weight
    part_of = lambda t, core: gw_all.at[pl.ds(pl.multiple_of(t * 32 + core * 16, 16), 16), :]
    part_at = gw_parts.at[rows(c * NZ + z, 16), :]

    def cross(t):
        copy(part_of(t, 1 - c), part_at, zs.at[ACROSS], zr.at[ACROSS], across(t)).start()

    def both(t):
        copy(part_of(t, c), part_at, zs.at[WEIGHT], zr.at[WEIGHT], z_dev(t)).start()
        cross(t)

    z_each(both)
    cross(z)
    gw_parts[rows(c * NZ + z, 16), :] = gw_all[pl.ds(pl.multiple_of(z * 32 + c * 16, 16), 16), :]
    z_drain(TURNED, turned, 32)
    p_drain(PROJ[0], gpall, BLOCK)
    p_drain(PROJ[1], gpall, BLOCK)

    z_recv(OWNERS, gs_in, 8)
    gp = jnp.concatenate([gs_in[e * 8:e * 8 + OWN, :] for e in range(SPLIT)], axis=1).astype(BF16)
    for j in range(H // TILE):
        here = slice(j * TILE, (j + 1) * TILE)
        gs_ref[:, here] = lax.dot_general(gp, w[here, :], NT, preferred_element_type=F32).astype(BF16)
    z_drain(OWNERS, gs_out, 8)
    eight = gw_parts.at[0:NZ * 16, :]
    crossed = copy(eight, eight, zs.at[ACROSS], zr.at[ACROSS], partner)
    z_recv(WEIGHT, gw_parts, 16)
    crossed.wait_recv()
    for e in range(SPLIT):
        gw_ref[:, e * LANES:(e + 1) * LANES] = (
            gw_parts[e * 16:(e + 1) * 16, :] + gw_parts[(NZ + e) * 16:(NZ + e + 1) * 16, :])
    z_drain(WEIGHT, gw_all, 16)
    crossed.wait_send()


def hand_over(loss_in, top_in, gs_in, gw_in, loss_ref, top_ref, gs_ref, gw_ref):
    loss_ref[...] = loss_in[0:1, 0:1]
    top_ref[...] = top_in[0:1, 0:OWN]
    gs_ref[...] = gs_in[...]
    gw_ref[...] = gw_in[...]


def local(states, head_weight, bank, positive_index):
    vmem = pltpu.VMEM
    dma = pltpu.SemaphoreType.DMA
    in_vmem = pl.BlockSpec(memory_space=pltpu.VMEM)
    grads = (jax.ShapeDtypeStruct((OWN, H), BF16), jax.ShapeDtypeStruct((16, E), F32))
    parts = pl.pallas_call(
        kernel,
        out_shape=(jax.ShapeDtypeStruct((8, LANES), F32),) * 2 + grads,
        in_specs=[
            in_vmem,
            pl.BlockSpec(memory_space=pl.ANY),
            pl.BlockSpec(memory_space=pl.ANY),
            pl.BlockSpec(memory_space=pltpu.SMEM),
        ],
        out_specs=(in_vmem,) * 4,
        scratch_shapes=[
            vmem((H, E), BF16),
            vmem((2 * BANK, E), BF16),
            vmem((NZ * 8, LANES), jnp.int32),
            vmem((PLANE * 8, LANES), jnp.int32),
            vmem((NZ * 16, LANES), F32),
            vmem((NZ * 16, LANES), F32),
            vmem((NY * 32, LANES), BF16),
            vmem((ROWS, LANES), BF16),
            vmem((NZ * 32, ROWS), BF16),
            vmem((LANES, SET), F32),
            vmem((NZ * OWN * SPLIT, LANES), BF16),
            vmem((NZ * OWN * SPLIT, LANES), F32),
            vmem((OWN * SPLIT, LANES), F32),
            vmem((NZ * 8, LANES), F32),
            vmem((NZ * 8, LANES), F32),
            vmem((SETS * NY, NX, 2, BLOCK, HALF), BF16),
            vmem((SET, 2 * BANK), F32),
            vmem((ROWS, 2 * BANK), BF16),
            vmem((ROWS, E), F32),
            vmem((ROWS, E), BF16),
            vmem((SETS * PLANE * 8, LANES), F32),
            vmem((SETS * NZ * 8, LANES), F32),
            vmem((24, LANES), F32),
            vmem((ROWS, E), BF16),
            vmem((ROWS, E), BF16),
            vmem((SETS * NZ * 24, LANES), F32),
            vmem((SETS * NZ * 24, LANES), F32),
            vmem((NZ * 8, LANES), F32),
            vmem((NZ * 8, LANES), F32),
            vmem((ROWS, LANES), BF16),
            vmem((NZ * 32, LANES), F32),
            vmem((2 * NZ * 16, LANES), F32),
            vmem((16, LANES), F32),
            dma((W_PARTS,)), dma,
            dma((2,)), dma((2,)),
            dma((STAGES,)), dma((STAGES,)),
            dma((STAGES,)), dma((STAGES,)),
            dma((SETS, NX + NY)),
        ],
        compiler_params=pltpu.CompilerParams(
            collective_id=0, has_side_effects=True, vmem_limit_bytes=56 * 2**20
        ),
        name="info_nce",
    )(states, head_weight, bank, positive_index)
    loss, top, grad_states, grad_weight = pl.pallas_call(
        hand_over,
        out_shape=(jax.ShapeDtypeStruct((1, 1), F32), jax.ShapeDtypeStruct((1, OWN), F32)) + grads,
        in_specs=[in_vmem] * 4,
        out_specs=(in_vmem,) * 4,
        name="hand_over",
    )(*parts)
    return (loss.reshape(()), top.reshape((OWN,)), grad_states, grad_weight)


def solution(mesh):
    placed = (P("dev", None), P(), P("dev", None), P("dev"))
    return jax.shard_map(
        local,
        mesh=mesh,
        in_specs=placed,
        out_specs=(P(), P("dev"), P("dev", None), P("dev", None)),
        check_vma=False,
    )
```
